256 devices in a mesh: tm: 4 (over z_hi), strip: 64 (over z_lo, y, x, core).
Axes of the slice: x: 4, y: 4, z: 8 (z_hi: 4, z_lo: 2; z = z_hi * 2 + z_lo), core: 2. Of those that a mesh axis runs over, the one named last changes fastest.
Arguments:
- density: float32 [4096, 512], P('strip'), may hold values from 0.05 to 0.95
- speed: float32 [4096, 512], P('strip'), may hold values from 0.3 to 1
- codes: int32 [4096, 512], P('strip'), may hold values from 0 to 7
- obstacle: int32 [4096, 512], P('strip'), may hold values 0 or 1
Outputs:
- slice_ends: float32 [4, 4096, 512], P('tm', 'strip')
The draws below stay inside these ranges and needn't reach their ends.
All inputs are finite; a program needn't handle non-finite values. No bound on the sum of `obstacle` on one device may be relied on, other than what follows from the above.
Results may differ from the reference program's by a relative error of at most 0.00002.
Values sent between devices are 32-bit elements; how exact they have to be, the bound alone decides.
No kernel may reach another device: no remote copies, remote signals or barrier semaphores. Data moves between devices by JAX's collectives and lax.ppermute only.
A program may use at most 64 MiB of HBM per device.

```python
import math
import jax
import jax.numpy as jnp
from jax import lax

NCOL = 512
FINE = 8
ITERS = 1
CSTEPS = 4
ROWS = 4096
N_SLICES = 4


def with_ends(values, own_key, smallest, top_value):
    extent = values.shape
    index_at = [jax.random.randint(jax.random.fold_in(own_key, axis), (), 0, extent[axis]) for axis in range(len(extent))]
    values = values.at[tuple(index_at)].set(smallest)
    longest = extent.index(max(extent))
    index_at[longest] = (index_at[longest] + 1) % extent[longest]
    return values.at[tuple(index_at)].set(top_value)


def block_scale(key, shape, pieces, smallest, high):
    def one(position, parts):
        draws = jax.random.uniform(jax.random.fold_in(jax.random.fold_in(key, 6), position), (parts,), jnp.float32, smallest / len(pieces), high / len(pieces))
        return jnp.repeat(jnp.exp(draws), shape[position] // parts).reshape((-1,) + (1,) * (len(shape) - position - 1))

    factor_of = one(*pieces[0])
    for cut in pieces[1:]:
        factor_of = factor_of * one(*cut)
    return factor_of


def setup_inputs(seed: int = 0) -> dict:
    arg_keys = jax.random.split(jax.random.key(seed), 5)
    density = jnp.clip(0.05 + 0.9 * jax.random.uniform(arg_keys[0], (ROWS, NCOL), jnp.float32) ** block_scale(arg_keys[0], (ROWS, NCOL), ((0, 64),), -0.2, 0.2), 0.05, 0.95)
    speed = jnp.clip(jnp.exp(math.log(1.0) - 1.2039728 * jax.random.uniform(arg_keys[1], (ROWS, NCOL), jnp.float32) ** block_scale(arg_keys[1], (ROWS, NCOL), ((0, 64),), -0.2, 0.2)), 0.3, 1.0)
    codes = with_ends(jax.random.randint(arg_keys[2], (ROWS, NCOL), 0, 8), jax.random.fold_in(arg_keys[2], 1), 0, 7).astype(jnp.int32)
    obstacle = with_ends((jax.random.randint(arg_keys[3], (ROWS, NCOL), 0, 8) < 1).astype(jnp.int32), jax.random.fold_in(arg_keys[3], 1), 0, 1)
    return {"density": density, "speed": speed, "codes": codes, "obstacle": obstacle}


OFFSETS = ((0, 1), (-1, 1), (-1, 0), (-1, -1), (0, -1), (1, -1), (1, 0), (1, 1))
LAMBDA = 0.9


def shifted(array, row_step, col_step):
    height, breadth = array.shape
    padded = jnp.pad(array, 1)
    return padded[1 + row_step:1 + row_step + height, 1 + col_step:1 + col_step + breadth]


def prepare(indicators, opening):
    count = jnp.zeros_like(opening)
    for d in range(8):
        count = count + shifted(indicators[d] * opening, -OFFSETS[d][0], -OFFSETS[d][1])
    return opening / jnp.maximum(count, 1.0)


def advance(field, push_rate, indicators, weight):
    pushed = push_rate * field
    room = (1.0 - field) * weight
    leaving = jnp.zeros_like(field)
    arriving = jnp.zeros_like(field)
    for d in range(8):
        leaving = leaving + indicators[d] * shifted(room, OFFSETS[d][0], OFFSETS[d][1])
        arriving = arriving + shifted(pushed * indicators[d], -OFFSETS[d][0], -OFFSETS[d][1])
    return field - pushed * leaving + room * arriving


def halve(array):
    return 0.25 * (((array[0::2, 0::2] + array[1::2, 0::2]) + array[0::2, 1::2]) + array[1::2, 1::2])


def double(array):
    return jnp.repeat(jnp.repeat(array, 2, axis=0), 2, axis=1)


def make_level(push_rate, codes, opening):
    indicators = [(codes == d).astype(jnp.float32) for d in range(8)]
    return push_rate, indicators, prepare(indicators, opening)


def run_steps(field, level, steps):
    push_rate, indicators, weight = level

    def one_step(index, current):
        return advance(current, push_rate, indicators, weight)

    return lax.fori_loop(0, steps, one_step, field)


def reference(density, speed, codes, obstacle):
    opening = 1.0 - obstacle.astype(jnp.float32)
    push_rate = LAMBDA * speed * opening
    start = density * opening
    fine_level = make_level(push_rate, codes, opening)
    coarse_level = make_level(halve(push_rate), codes[0::2, 0::2], halve(opening))

    def coarse_of(field):
        return run_steps(halve(field), coarse_level, CSTEPS)

    starts = [start]
    previous = []
    for n in range(N_SLICES):
        guess = coarse_of(starts[n])
        previous.append(guess)
        starts.append(double(guess))
    for k in range(ITERS):
        refined = [run_steps(starts[n], fine_level, FINE) for n in range(N_SLICES)]
        fresh = [start]
        current = []
        for n in range(N_SLICES):
            guess = coarse_of(fresh[n])
            current.append(guess)
            fresh.append(refined[n] + double(guess - previous[n]))
        starts = fresh
        previous = current
    return jnp.stack(starts[1:])
```

```python
import jax
import jax.numpy as jnp
from jax import lax
from jax.experimental import pallas as pl
from jax.experimental.pallas import tpu as pltpu
from jax.sharding import PartitionSpec as P

FINE = 8
CSTEPS = 4
LAMBDA = 0.9
OFFSETS = ((0, 1), (-1, 1), (-1, 0), (-1, -1), (0, -1), (1, -1), (1, 0), (1, 1))

LANES = 128
TILES = 4
HEIGHT = 64
HALO = 32
WINDOW = HEIGHT + 2 * HALO
ROWS_F = WINDOW // 8
ROWS_C = ROWS_F // 2
TILES_C = TILES // 2
SENT = 3 * HALO + 8


def lane_ids():
    return lax.broadcasted_iota(jnp.int32, (8, LANES), 1)


def sublane_ids():
    return lax.broadcasted_iota(jnp.int32, (8, LANES), 0)


def interleave(tiles):
    lane = lane_ids()
    result = []
    for t in range(TILES):
        index = (lane * TILES + t) % LANES
        picked = [jnp.take_along_axis(tile, index, axis=1) for tile in tiles]
        merged = picked[3]
        for j in (2, 1, 0):
            merged = jnp.where(lane < 32 * (j + 1), picked[j], merged)
        result.append(merged)
    return result


def deinterleave(tiles):
    lane = lane_ids()
    part = lane % TILES
    result = []
    for j in range(TILES):
        index = lane // TILES + 32 * j
        picked = [jnp.take_along_axis(tile, index, axis=1) for tile in tiles]
        merged = picked[3]
        for t in (2, 1, 0):
            merged = jnp.where(part == t, picked[t], merged)
        result.append(merged)
    return result


def prep_kernel(density, speed, codes, obstacle, own, to_next, to_prev):
    for block in range(HEIGHT // 8):
        rows = pl.ds(8 * block, 8)
        cols = [pl.ds(LANES * j, LANES) for j in range(TILES)]
        opening = [1.0 - obstacle[rows, c].astype(jnp.float32) for c in cols]
        rate = [LAMBDA * speed[rows, c] * o for c, o in zip(cols, opening)]
        start = [density[rows, c] * o for c, o in zip(cols, opening)]
        code = [codes[rows, c].astype(jnp.float32) for c in cols]
        for field, tiles in enumerate((rate, code, start)):
            for t, value in enumerate(interleave(tiles)):
                own[t, pl.ds(HEIGHT * field + 8 * block, 8), :] = value
                if block < 4:
                    to_prev[t, pl.ds(HALO * field + 8 * block, 8), :] = value
                else:
                    to_next[t, pl.ds(HALO * field + 8 * (block - 4), 8), :] = value
    for t in range(TILES):
        for target in (to_next, to_prev):
            target[t, pl.ds(3 * HALO, 8), :] = jnp.zeros((8, LANES), jnp.float32)
        for place, (field, row) in enumerate(((0, 31), (0, 30), (1, 31), (1, 30))):
            to_next[t, pl.ds(3 * HALO + place, 1), :] = own[t, pl.ds(HEIGHT * field + row, 1), :]
        for place, (field, row) in enumerate(((0, 32), (0, 33), (1, 32), (1, 33))):
            to_prev[t, pl.ds(3 * HALO + 7 - place, 1), :] = own[t, pl.ds(HEIGHT * field + row, 1), :]


def from_left(tile):
    return jnp.where(lane_ids() == 0, 0.0, pltpu.roll(tile, 1, 1))


def from_right(tile):
    return jnp.where(lane_ids() == LANES - 1, 0.0, pltpu.roll(tile, LANES - 1, 1))


def from_above(tile):
    return jnp.where(sublane_ids() == 0, 0.0, pltpu.roll(tile, 1, 0))


def from_below(tile):
    return jnp.where(sublane_ids() == 7, 0.0, pltpu.roll(tile, 7, 0))


def sweep(rows, tiles, code_at, amount_at, emit, outside=()):
    sums = {}

    def add(r, t, value):
        sums[r, t] = sums[r, t] + value if (r, t) in sums else value

    def finish(r):
        add(r, 0, from_left(sums.pop((r, tiles))))
        add(r, tiles - 1, from_right(sums.pop((r, -1))))
        for t in range(tiles):
            emit(r, t, sums.pop((r, t)))

    for r, row_step, codes, amounts in outside:
        for t in range(tiles):
            for d, (dr, dc) in enumerate(OFFSETS):
                if dr == row_step:
                    add(r + dr, t + dc, jnp.where(codes[t] == float(d), amounts[t], 0.0))
    for r in range(rows):
        for t in range(tiles):
            code = code_at(r, t)
            masks = [code == float(d) for d in range(8)]
            kept, flow = amount_at(r, t, masks)
            if kept is not None:
                add(r, t, kept)
            for mask, (dr, dc) in zip(masks, OFFSETS):
                add(r + dr, t + dc, jnp.where(mask, flow, 0.0))
        if r >= 2:
            finish(r - 1)
    for t in range(-1, tiles + 1):
        add(rows - 1, t, from_below(sums.pop((-1, t))))
        add(0, t, from_above(sums.pop((rows, t))))
    finish(rows - 1)
    finish(0)


def advance(rows, tiles, rho, rate, code, weight):
    field, room = {}, {}

    def load(r):
        for t in range(tiles):
            field[r, t] = rho[r * tiles + t]
            room[r, t] = (1.0 - field[r, t]) * weight[r * tiles + t]
        room[r, -1] = from_left(room[r, tiles - 1])
        room[r, tiles] = from_right(room[r, 0])

    load(rows - 1)
    load(0)
    for t in range(-1, tiles + 1):
        room[-1, t] = from_above(room[rows - 1, t])
        room[rows, t] = from_below(room[0, t])

    def amount_at(r, t, masks):
        if t == 0 and r + 1 < rows - 1:
            load(r + 1)
        leaving = room[r + OFFSETS[0][0], t + OFFSETS[0][1]]
        for mask, (dr, dc) in zip(masks[1:], OFFSETS[1:]):
            leaving = jnp.where(mask, room[r + dr, t + dc], leaving)
        flow = rate[r * tiles + t] * field[r, t] * leaving
        return field[r, t] - flow, flow

    def emit(r, t, value):
        rho[r * tiles + t] = value

    sweep(rows, tiles, lambda r, t: code[r * tiles + t], amount_at, emit)


def fine_at(r, t):
    return r * TILES + t


def coarse_at(r, t):
    return r * TILES_C + t


def halved(get):
    return [
        0.25 * (((get(2 * r, 2 * t) + get(2 * r + 1, 2 * t)) + get(2 * r, 2 * t + 1)) + get(2 * r + 1, 2 * t + 1))
        for r in range(ROWS_C)
        for t in range(TILES_C)
    ]


def main_kernel(
    own, low, high, out, win, ext, rate, code, weight, rho, crate, ccode, cweight, guess, fresh, sems
):
    copies = []

    def copy(source, target):
        copies.append(pltpu.make_async_copy(source, target, sems.at[len(copies)]))
        copies[-1].start()

    for field in range(3):
        copy(low.at[:, pl.ds(HALO * field, HALO), :], win.at[field, :, pl.ds(0, HALO), :])
        copy(own.at[:, pl.ds(HEIGHT * field, HEIGHT), :], win.at[field, :, pl.ds(HALO, HEIGHT), :])
        copy(high.at[:, pl.ds(HALO * field, HALO), :], win.at[field, :, pl.ds(HALO + HEIGHT, HALO), :])
    copy(low.at[:, pl.ds(3 * HALO, 8), :], ext.at[0])
    copy(high.at[:, pl.ds(3 * HALO, 8), :], ext.at[1])
    for item in copies:
        item.wait()

    for r in range(ROWS_F):
        for t in range(TILES):
            rows = pl.ds(r, 8, stride=ROWS_F)
            rate[fine_at(r, t)] = win[0, t, rows, :]
            code[fine_at(r, t)] = win[1, t, rows, :]
            rho[fine_at(r, t)] = win[2, t, rows, :]

    def is_open(value):
        return jnp.where(value > 0.0, 1.0, 0.0)

    def weigh(target, index):
        def emit(r, t, count):
            target[index(r, t)] = target[index(r, t)] / jnp.maximum(count, 1.0)

        return emit

    for i in range(ROWS_F * TILES):
        weight[i] = is_open(rate[i])
    for i, value in enumerate(halved(lambda r, t: weight[fine_at(r, t)])):
        cweight[i] = value
    for i, value in enumerate(halved(lambda r, t: rate[fine_at(r, t)])):
        crate[i] = value
    for r in range(ROWS_C):
        for t in range(TILES_C):
            ccode[coarse_at(r, t)] = code[fine_at(2 * r, 2 * t)]

    fine_out, coarse_out = [], []
    for side, (edge, step, last_f, last_c) in enumerate(((0, 1, -1, -1), (7, -1, ROWS_F, ROWS_C))):
        at_edge = sublane_ids() == edge
        turn = (lambda x, n: pltpu.roll(x, (8 - n) % 8, 0)) if side == 0 else (lambda x, n: pltpu.roll(x, n, 0))
        tile = [ext[side, t] for t in range(TILES)]
        near = [jnp.where(at_edge, is_open(x), 0.0) for x in tile]
        far = [jnp.where(at_edge, is_open(turn(x, 1)), 0.0) for x in tile]
        near_code = [turn(x, 2) for x in tile]
        far_code = [turn(x, 3) for x in tile]
        even_code = far_code if side == 0 else near_code
        mean = [
            0.25 * (((near[2 * t] + far[2 * t]) + near[2 * t + 1]) + far[2 * t + 1]) for t in range(TILES_C)
        ]
        fine_out.append((last_f, step, near_code, near))
        coarse_out.append((last_c, step, [even_code[2 * t] for t in range(TILES_C)], mean))

    sweep(
        ROWS_F, TILES, lambda r, t: code[fine_at(r, t)],
        lambda r, t, masks: (None, is_open(rate[fine_at(r, t)])), weigh(weight, fine_at), fine_out,
    )
    opening_c = [cweight[i] for i in range(ROWS_C * TILES_C)]
    sweep(
        ROWS_C, TILES_C, lambda r, t: ccode[coarse_at(r, t)],
        lambda r, t, masks: (None, opening_c[coarse_at(r, t)]), weigh(cweight, coarse_at), coarse_out,
    )

    n = lax.axis_index("tm")

    def run_fine():
        @pl.loop(0, FINE)
        def _(step):
            advance(ROWS_F, TILES, rho, rate, code, weight)

    def run_coarse(*fields):
        @pl.loop(0, CSTEPS)
        def _(step):
            for item in fields:
                advance(ROWS_C, TILES_C, item, crate, ccode, cweight)

    @pl.when(n > 0)
    def _():
        for i, value in enumerate(halved(lambda r, t: rho[fine_at(r, t)])):
            guess[i] = value
        run_coarse(guess)

    run_fine()
    for i in range(ROWS_C * TILES_C):
        fresh[i] = jnp.zeros((8, LANES), jnp.float32)

    @pl.loop(1, n + 1)
    def _(m):
        for i, value in enumerate(halved(lambda r, t: rho[fine_at(r, t)])):
            fresh[i] = value + fresh[i]
        for r in range(ROWS_F):
            for t in range(TILES):
                rho[fine_at(r, t)] = guess[coarse_at(r // 2, t // 2)]
        run_fine()
        run_coarse(guess, fresh)
        for i in range(ROWS_C * TILES_C):
            fresh[i] = fresh[i] - guess[i]

    for r in range(ROWS_F):
        for t in range(TILES):
            win[0, t, pl.ds(r, 8, stride=ROWS_F), :] = rho[fine_at(r, t)] + fresh[coarse_at(r // 2, t // 2)]
    for block in range(HEIGHT // 8):
        rows = pl.ds(HALO + 8 * block, 8)
        for j, value in enumerate(deinterleave([win[0, t, rows, :] for t in range(TILES)])):
            out[pl.ds(8 * block, 8), pl.ds(LANES * j, LANES)] = value


def per_device(density, speed, codes, obstacle):
    f32 = jnp.float32
    own, to_next, to_prev = pl.pallas_call(
        prep_kernel,
        out_shape=(
            jax.ShapeDtypeStruct((TILES, 3 * HEIGHT, LANES), f32),
            jax.ShapeDtypeStruct((TILES, SENT, LANES), f32),
            jax.ShapeDtypeStruct((TILES, SENT, LANES), f32),
        ),
        name="prep",
    )(density, speed, codes, obstacle)
    count = lax.axis_size("strip")
    forward = [(i, i + 1) for i in range(count - 1)]
    backward = [(target, source) for source, target in forward]
    low = lax.ppermute(to_next, "strip", forward)
    high = lax.ppermute(to_prev, "strip", backward)
    fine = pltpu.VMEM((ROWS_F * TILES, 8, LANES), f32)
    coarse = pltpu.VMEM((ROWS_C * TILES_C, 8, LANES), f32)
    result = pl.pallas_call(
        main_kernel,
        out_shape=jax.ShapeDtypeStruct((HEIGHT, TILES * LANES), f32),
        in_specs=[pl.BlockSpec(memory_space=pl.ANY)] * 3,
        scratch_shapes=[
            pltpu.VMEM((3, TILES, WINDOW, LANES), f32),
            pltpu.VMEM((2, TILES, 8, LANES), f32),
            fine, fine, fine, fine,
            coarse, coarse, coarse, coarse, coarse,
            pltpu.SemaphoreType.DMA((11,)),
        ],
        compiler_params=pltpu.CompilerParams(vmem_limit_bytes=32 * 1024 * 1024),
        name="parareal",
    )(own, low, high)
    return result[None]


def solution(mesh):
    in_specs = (P("strip", None), P("strip", None), P("strip", None), P("strip", None))
    out_specs = P("tm", "strip", None)
    return jax.shard_map(
        per_device, mesh=mesh, in_specs=in_specs, out_specs=out_specs, check_vma=False
    )
```

```python
import jax
import jax.numpy as jnp
from jax import lax
from jax.experimental import pallas as pl
from jax.experimental.pallas import tpu as pltpu
from jax.sharding import PartitionSpec as P

FINE = 8
CSTEPS = 4
LAMBDA = 0.9
OFFSETS = ((0, 1), (-1, 1), (-1, 0), (-1, -1), (0, -1), (1, -1), (1, 0), (1, 1))

LANES = 128
TILES = 4
TILES_C = TILES // 2
HEIGHT = 64
HALO = 32
MARGIN = 40
SPAN = HEIGHT + 2 * MARGIN
SENT = 3 * HALO + 8
STAGES = ((6, 18), (16, 14), (24, 12), (32, 10))
SPAN_C = 8 * STAGES[0][1] // 2


def lane_ids():
    return lax.broadcasted_iota(jnp.int32, (8, LANES), 1)


def sublane_ids():
    return lax.broadcasted_iota(jnp.int32, (8, LANES), 0)


def interleave(tiles):
    lane = lane_ids()
    result = []
    for t in range(TILES):
        index = (lane * TILES + t) % LANES
        picked = [jnp.take_along_axis(tile, index, axis=1) for tile in tiles]
        merged = picked[3]
        for j in (2, 1, 0):
            merged = jnp.where(lane < 32 * (j + 1), picked[j], merged)
        result.append(merged)
    return result


def deinterleave(tiles):
    lane = lane_ids()
    part = lane % TILES
    result = []
    for j in range(TILES):
        index = lane // TILES + 32 * j
        picked = [jnp.take_along_axis(tile, index, axis=1) for tile in tiles]
        merged = picked[3]
        for t in (2, 1, 0):
            merged = jnp.where(part == t, picked[t], merged)
        result.append(merged)
    return result


def products(density, speed, codes, obstacle, rows):
    cols = [pl.ds(LANES * j, LANES) for j in range(TILES)]
    opening = [1.0 - obstacle[rows, c].astype(jnp.float32) for c in cols]
    rate = [LAMBDA * speed[rows, c] * o for c, o in zip(cols, opening)]
    start = [density[rows, c] * o for c, o in zip(cols, opening)]
    code = [codes[rows, c].astype(jnp.float32) for c in cols]
    return rate, code, start


def edge_tile(rate, code, to_next):
    s = sublane_ids()
    below = jnp.where(s >= 6, rate, pltpu.roll(code, 6, 0))
    above = jnp.where(s < 2, rate, pltpu.roll(code, 2, 0))
    return jnp.where(to_next, below, above)


def cross_kernel(density, speed, codes, obstacle, sent, d_buf, s_buf, c_buf, o_buf, sems):
    odd = lax.axis_index("strip") % 2
    rows = pl.ds(pl.multiple_of(24 * odd, 8), 40)
    bufs = (d_buf, s_buf, c_buf, o_buf)
    copies = [
        pltpu.make_async_copy(source.at[rows, :], buf, sems.at[i])
        for i, (source, buf) in enumerate(zip((density, speed, codes, obstacle), bufs))
    ]
    for item in copies:
        item.start()
    for item in copies:
        item.wait()
    for block in range(4):
        fields = products(*bufs, pl.ds(pl.multiple_of(8 * (block + odd), 8), 8))
        for field, tiles in enumerate(fields):
            for t, value in enumerate(tiles):
                sent[t, pl.ds(HALO * field + 8 * block, 8), :] = value
    rate, code, _ = products(*bufs, pl.ds(pl.multiple_of(32 * (1 - odd), 8), 8))
    for t in range(TILES):
        sent[t, pl.ds(3 * HALO, 8), :] = edge_tile(rate[t], code[t], odd == 1)


def own_kernel(density, speed, codes, obstacle, own, sent):
    even = lax.axis_index("strip") % 2 == 0
    for block in range(HEIGHT // 8):
        fields = products(density, speed, codes, obstacle, pl.ds(8 * block, 8))
        for field, tiles in enumerate(fields):
            for t, value in enumerate(interleave(tiles)):
                own[t, pl.ds(HEIGHT * field + 8 * block, 8), :] = value
    for t in range(TILES):
        for field in range(3):
            for block in range(4):
                first, second = (own[t, pl.ds(HEIGHT * field + 8 * b, 8), :] for b in (block, block + 4))
                sent[t, pl.ds(HALO * field + 8 * block, 8), :] = jnp.where(even, second, first)
        rate, code = (
            jnp.where(even, own[t, pl.ds(HEIGHT * field + 24, 8), :], own[t, pl.ds(HEIGHT * field + 32, 8), :])
            for field in range(2)
        )
        sent[t, pl.ds(3 * HALO, 8), :] = edge_tile(rate, code, even)


def from_left(tile):
    return jnp.where(lane_ids() == 0, 0.0, pltpu.roll(tile, 1, 1))


def from_right(tile):
    return jnp.where(lane_ids() == LANES - 1, 0.0, pltpu.roll(tile, LANES - 1, 1))


def from_above(tile):
    return jnp.where(sublane_ids() == 0, 0.0, pltpu.roll(tile, 1, 0))


def from_below(tile):
    return jnp.where(sublane_ids() == 7, 0.0, pltpu.roll(tile, 7, 0))


def sweep(rows, tiles, amounts_at, emit):
    sums = {}

    def add(r, t, value):
        sums[r, t] = sums[r, t] + value if (r, t) in sums else value

    def finish(r):
        add(r, 0, from_left(sums.pop((r, tiles))))
        add(r, tiles - 1, from_right(sums.pop((r, -1))))
        for t in range(tiles):
            emit(r, t, sums.pop((r, t)))

    for r in range(rows):
        for t in range(tiles):
            kept, flows = amounts_at(r, t)
            if kept is not None:
                add(r, t, kept)
            for flow, (dr, dc) in zip(flows, OFFSETS):
                add(r + dr, t + dc, flow)
        if r >= 2:
            finish(r - 1)
    for t in range(-1, tiles + 1):
        add(rows - 1, t, from_below(sums.pop((-1, t))))
        add(0, t, from_above(sums.pop((rows, t))))
    finish(rows - 1)
    finish(0)


def picked(bits, values):
    for bit in bits:
        values = [jnp.where(bit, odd, even) for even, odd in zip(values[0::2], values[1::2])]
    return values[0]


class Level:
    def __init__(self, first, rows, tiles, rate, parts, bits, weight):
        self.first, self.rows, self.tiles = first, rows, tiles
        self.rate, self.parts, self.bits, self.weight = rate, parts, bits, weight

    def at(self, r, t):
        return r * self.tiles + t

    def cells(self):
        return [(r, t) for r in range(self.rows) for t in range(self.tiles)]

    def line(self, r):
        return pl.ds(self.first + r, 8, stride=self.rows)

    def get(self, ref, r, t):
        return ref[t, self.line(r), :]

    def put(self, ref, r, t, value):
        ref[t, self.line(r), :] = value

    def fill(self, rate_at, code_at, opening_at):
        opening = {}

        def amounts_at(r, t):
            rate, code = rate_at(r, t), code_at(r, t)
            opening[r, t] = opening_at(r, t)
            masks = [code == float(d) for d in range(8)]
            for d, mask in enumerate(masks):
                self.put(self.parts.at[d], r, t, jnp.where(mask, rate, 0.0))
            number = code.astype(jnp.int32)
            for n in range(3):
                self.put(self.bits.at[n], r, t, number & (1 << n))
            return None, [jnp.where(mask, opening[r, t], 0.0) for mask in masks]

        def emit(r, t, count):
            self.put(self.weight, r, t, opening[r, t] / jnp.maximum(count, 1.0))

        sweep(self.rows, self.tiles, amounts_at, emit)

    def advance(self, rho):
        rows, tiles = self.rows, self.tiles
        field, room = {}, {}

        def load(r):
            for t in range(tiles):
                field[r, t] = rho[self.at(r, t)]
                room[r, t] = (1.0 - field[r, t]) * self.get(self.weight, r, t)
            room[r, -1] = from_left(room[r, tiles - 1])
            room[r, tiles] = from_right(room[r, 0])

        load(rows - 1)
        load(0)
        for t in range(-1, tiles + 1):
            room[-1, t] = from_above(room[rows - 1, t])
            room[rows, t] = from_below(room[0, t])

        def amounts_at(r, t):
            if t == 0 and r + 1 < rows - 1:
                load(r + 1)
            bits = [self.get(self.bits.at[n], r, t) != 0 for n in range(3)]
            leaving = picked(bits, [room[r + dr, t + dc] for dr, dc in OFFSETS])
            share = field[r, t] * leaving
            flows = [self.get(self.parts.at[d], r, t) * share for d in range(8)]
            return field[r, t] - self.get(self.rate, r, t) * share, flows

        def emit(r, t, value):
            rho[self.at(r, t)] = value

        sweep(rows, tiles, amounts_at, emit)


def halved(level, get):
    def at(r, t):
        r, t = 2 * r, 2 * t
        return 0.25 * (((get(r, t) + get(r + 1, t)) + get(r, t + 1)) + get(r + 1, t + 1))

    return {(r, t): at(r, t) for r, t in level.cells()}


def is_open(value):
    return jnp.where(value > 0.0, 1.0, 0.0)


def main_kernel(
    own, crossed, paired, out, rate, code, start, parts, bits, weight, rho,
    crate, cparts, cbits, cweight, guess, fresh, last_guess, last_fresh,
):
    even = lax.axis_index("strip") % 2 == 0
    fields = (rate, code, start)
    for i, field in enumerate(fields):
        for t in range(TILES):
            for block in range(HEIGHT // 8):
                field[t, pl.ds(MARGIN + 8 * block, 8), :] = own[t, pl.ds(HEIGHT * i + 8 * block, 8), :]

    zeros = jnp.zeros((8, LANES), jnp.float32)

    def place_halo(tiles_at, high):
        place = pl.multiple_of(jnp.where(high, MARGIN + HEIGHT, MARGIN - HALO), 8)
        beyond = pl.ds(pl.multiple_of(jnp.where(high, SPAN - 8, 0), 8), 8)
        for i, field in enumerate(fields):
            for block in range(HALO // 8):
                for t, tile in enumerate(tiles_at(HALO * i + 8 * block)):
                    field[t, pl.ds(place + 8 * block, 8), :] = tile
        s = sublane_ids()
        for t, tile in enumerate(tiles_at(3 * HALO)):
            there = jnp.where(high, s, 7 - s) < 2
            turned = jnp.where(high, pltpu.roll(tile, 6, 0), pltpu.roll(tile, 2, 0))
            rate[t, beyond, :] = jnp.where(there, tile, 0.0)
            code[t, beyond, :] = jnp.where(there, turned, 0.0)
            start[t, beyond, :] = zeros

    place_halo(lambda row: [paired[t, pl.ds(row, 8), :] for t in range(TILES)], even)
    place_halo(
        lambda row: interleave([crossed[t, pl.ds(row, 8), :] for t in range(TILES)]), jnp.logical_not(even)
    )
    for field in fields:
        for t in range(TILES):
            field[t, pl.ds(SPAN, 8), :] = zeros

    stages = [
        (
            Level(first, rows, TILES, rate, parts, bits, weight),
            Level((first - STAGES[0][0]) // 2, rows // 2, TILES_C, crate, cparts, cbits, cweight),
        )
        for first, rows in STAGES
    ]
    fine, coarse = stages[0]
    rates, openings = {}, {}

    def rate_at(r, t):
        rates[r, t] = fine.get(rate, r, t)
        openings[r, t] = is_open(rates[r, t])
        return rates[r, t]

    fine.fill(rate_at, lambda r, t: fine.get(code, r, t), lambda r, t: openings[r, t])
    mean_rate = halved(coarse, lambda r, t: fine.get(rate, r, t))
    mean_open = halved(coarse, lambda r, t: is_open(fine.get(rate, r, t)))
    for (r, t), value in mean_rate.items():
        coarse.put(crate, r, t, value)
    coarse.fill(
        lambda r, t: mean_rate[r, t], lambda r, t: fine.get(code, 2 * r, 2 * t), lambda r, t: mean_open[r, t]
    )

    n = lax.axis_index("tm")

    def run_fine(level):
        @pl.loop(0, FINE)
        def _(step):
            level.advance(rho)

    def run_coarse(level, *items):
        @pl.loop(0, CSTEPS)
        def _(step):
            for item in items:
                level.advance(item)

    def finish(fine, coarse, change):
        def value(r, t):
            result = rho[fine.at(r, t)]
            return result if change is None else result + change[r // 2, t // 2]

        values = {(r, t): value(r, t) for r, t in fine.cells()}
        for (r, t), item in values.items():
            fine.put(start, r, t, item)
        for (r, t), item in halved(coarse, lambda r, t: values[r, t]).items():
            coarse.put(last_fresh, r, t, item)
            coarse.put(last_guess, r, t, guess[coarse.at(r, t)])

    for r, t in fine.cells():
        rho[fine.at(r, t)] = fine.get(start, r, t)

    @pl.when(n > 0)
    def _():
        for (r, t), value in halved(coarse, lambda r, t: rho[fine.at(r, t)]).items():
            guess[coarse.at(r, t)] = value
        run_coarse(coarse, guess)

    run_fine(fine)
    finish(fine, coarse, None)

    def stage(m):
        fine, coarse = stages[m]

        @pl.when(n >= m)
        def _():
            for r, t in coarse.cells():
                value = coarse.get(last_guess, r, t)
                guess[coarse.at(r, t)] = value
                for i in range(4):
                    rho[fine.at(2 * r + i // 2, 2 * t + i % 2)] = value
                fresh[coarse.at(r, t)] = coarse.get(last_fresh, r, t)
            run_fine(fine)
            run_coarse(coarse, guess, fresh)
            finish(fine, coarse, {(r, t): fresh[coarse.at(r, t)] - guess[coarse.at(r, t)] for r, t in coarse.cells()})

    for m in range(1, len(STAGES)):
        stage(m)

    for block in range(HEIGHT // 8):
        rows = pl.ds(MARGIN + 8 * block, 8)
        for j, value in enumerate(deinterleave([start[t, rows, :] for t in range(TILES)])):
            out[pl.ds(8 * block, 8), pl.ds(LANES * j, LANES)] = value


def per_device(density, speed, codes, obstacle):
    f32, i32 = jnp.float32, jnp.int32
    args = (density, speed, codes, obstacle)
    sent_shape = pltpu.VMEM((TILES, SENT, LANES), f32)
    to_cross = pl.pallas_call(
        cross_kernel,
        out_shape=sent_shape,
        in_specs=[pl.BlockSpec(memory_space=pl.ANY)] * 4,
        scratch_shapes=[pltpu.VMEM((40, TILES * LANES), x.dtype) for x in args] + [pltpu.SemaphoreType.DMA((4,))],
        name="cross",
    )(*args)
    count = lax.axis_size("strip")
    across = [(i, i + 1) for i in range(1, count - 1, 2)]
    within = [(i, i + 1) for i in range(0, count, 2)]
    crossed = lax.ppermute(to_cross, "strip", across + [(j, i) for i, j in across])
    own, to_pair = pl.pallas_call(
        own_kernel,
        out_shape=(pltpu.VMEM((TILES, 3 * HEIGHT, LANES), f32), sent_shape),
        cost_estimate=pl.CostEstimate(flops=10_000_000, bytes_accessed=2_000_000, transcendentals=0),
        name="own",
    )(*args)
    paired = lax.ppermute(to_pair, "strip", within + [(j, i) for i, j in within])

    fine_lines = (TILES, SPAN + 8, LANES)
    coarse_lines = (TILES_C, SPAN_C, LANES)
    fine_cells, coarse_cells = (pltpu.VMEM((SPAN_C * n // 8, 8, LANES), f32) for n in (2 * TILES, TILES_C))
    result = pl.pallas_call(
        main_kernel,
        out_shape=jax.ShapeDtypeStruct((HEIGHT, TILES * LANES), f32),
        in_specs=[pl.BlockSpec(memory_space=pltpu.VMEM)] * 3,
        scratch_shapes=[
            pltpu.VMEM(fine_lines, f32),
            pltpu.VMEM(fine_lines, f32),
            pltpu.VMEM(fine_lines, f32),
            pltpu.VMEM((8, *fine_lines), f32),
            pltpu.VMEM((3, *fine_lines), i32),
            pltpu.VMEM(fine_lines, f32),
            fine_cells,
            pltpu.VMEM(coarse_lines, f32),
            pltpu.VMEM((8, *coarse_lines), f32),
            pltpu.VMEM((3, *coarse_lines), i32),
            pltpu.VMEM(coarse_lines, f32),
            coarse_cells,
            coarse_cells,
            pltpu.VMEM(coarse_lines, f32),
            pltpu.VMEM(coarse_lines, f32),
        ],
        compiler_params=pltpu.CompilerParams(vmem_limit_bytes=32 * 1024 * 1024),
        name="parareal",
    )(own, crossed, paired)
    return result[None]


def solution(mesh):
    in_specs = (P("strip", None), P("strip", None), P("strip", None), P("strip", None))
    out_specs = P("tm", "strip", None)
    return jax.shard_map(
        per_device, mesh=mesh, in_specs=in_specs, out_specs=out_specs, check_vma=False
    )
```

```python
import jax
import jax.numpy as jnp
from jax import lax
from jax.experimental import pallas as pl
from jax.experimental.pallas import tpu as pltpu
from jax.sharding import PartitionSpec as P

FINE = 8
CSTEPS = 4
LAMBDA = 0.9
OFFSETS = ((0, 1), (-1, 1), (-1, 0), (-1, -1), (0, -1), (1, -1), (1, 0), (1, 1))

LANES = 128
TILES = 4
TILES_C = TILES // 2
HEIGHT = 64
HALO = 32
MARGIN = 40
SPAN = HEIGHT + 2 * MARGIN
SENT = 3 * HALO + 8
STAGES = ((7, 17), (16, 14), (24, 12), (32, 10))
STAGES_C = ((3, 9), (8, 7), (12, 6), (16, 5))
SPAN_C = (SPAN + 8) // 2


def lane_ids():
    return lax.broadcasted_iota(jnp.int32, (8, LANES), 1)


def sublane_ids():
    return lax.broadcasted_iota(jnp.int32, (8, LANES), 0)


def interleave(tiles):
    lane = lane_ids()
    result = []
    for t in range(TILES):
        index = (lane * TILES + t) % LANES
        picked = [jnp.take_along_axis(tile, index, axis=1) for tile in tiles]
        merged = picked[3]
        for j in (2, 1, 0):
            merged = jnp.where(lane < 32 * (j + 1), picked[j], merged)
        result.append(merged)
    return result


def deinterleave(tiles):
    lane = lane_ids()
    part = lane % TILES
    result = []
    for j in range(TILES):
        index = lane // TILES + 32 * j
        picked = [jnp.take_along_axis(tile, index, axis=1) for tile in tiles]
        merged = picked[3]
        for t in (2, 1, 0):
            merged = jnp.where(part == t, picked[t], merged)
        result.append(merged)
    return result


def products(density, speed, codes, obstacle, rows):
    cols = [pl.ds(LANES * j, LANES) for j in range(TILES)]
    opening = [1.0 - obstacle[rows, c].astype(jnp.float32) for c in cols]
    rate = [LAMBDA * speed[rows, c] * o for c, o in zip(cols, opening)]
    start = [density[rows, c] * o for c, o in zip(cols, opening)]
    code = [codes[rows, c].astype(jnp.float32) for c in cols]
    return rate, code, start


def edge_tile(rate, code, to_next):
    s = sublane_ids()
    below = jnp.where(s >= 6, rate, pltpu.roll(code, 6, 0))
    above = jnp.where(s < 2, rate, pltpu.roll(code, 2, 0))
    return jnp.where(to_next, below, above)


def cross_kernel(density, speed, codes, obstacle, sent, d_buf, s_buf, c_buf, o_buf, sems):
    odd = lax.axis_index("strip") % 2
    rows = pl.ds(pl.multiple_of(24 * odd, 8), 40)
    bufs = (d_buf, s_buf, c_buf, o_buf)
    copies = [
        pltpu.make_async_copy(source.at[rows, :], buf, sems.at[i])
        for i, (source, buf) in enumerate(zip((density, speed, codes, obstacle), bufs))
    ]
    for item in copies:
        item.start()
    for item in copies:
        item.wait()
    for block in range(4):
        fields = products(*bufs, pl.ds(pl.multiple_of(8 * (block + odd), 8), 8))
        for field, tiles in enumerate(fields):
            for t, value in enumerate(tiles):
                sent[t, pl.ds(HALO * field + 8 * block, 8), :] = value
    rate, code, _ = products(*bufs, pl.ds(pl.multiple_of(32 * (1 - odd), 8), 8))
    for t in range(TILES):
        sent[t, pl.ds(3 * HALO, 8), :] = edge_tile(rate[t], code[t], odd == 1)


def own_kernel(density, speed, codes, obstacle, own, sent):
    even = lax.axis_index("strip") % 2 == 0
    for block in range(HEIGHT // 8):
        fields = products(density, speed, codes, obstacle, pl.ds(8 * block, 8))
        for field, tiles in enumerate(fields):
            for t, value in enumerate(interleave(tiles)):
                own[t, pl.ds(HEIGHT * field + 8 * block, 8), :] = value
    for t in range(TILES):
        for field in range(3):
            for block in range(4):
                first, second = (own[t, pl.ds(HEIGHT * field + 8 * b, 8), :] for b in (block, block + 4))
                sent[t, pl.ds(HALO * field + 8 * block, 8), :] = jnp.where(even, second, first)
        rate, code = (
            jnp.where(even, own[t, pl.ds(HEIGHT * field + 24, 8), :], own[t, pl.ds(HEIGHT * field + 32, 8), :])
            for field in range(2)
        )
        sent[t, pl.ds(3 * HALO, 8), :] = edge_tile(rate, code, even)


def from_left(tile):
    return pltpu.roll(tile, 1, 1)


def from_right(tile):
    return pltpu.roll(tile, LANES - 1, 1)


def from_above(tile):
    return jnp.where(sublane_ids() == 0, 0.0, pltpu.roll(tile, 1, 0))


def from_below(tile):
    return jnp.where(sublane_ids() == 7, 0.0, pltpu.roll(tile, 7, 0))


def sweep(rows, tiles, amounts_at, emit):
    sums = {}

    def add(r, t, value):
        sums[r, t] = sums[r, t] + value if (r, t) in sums else value

    def finish(r):
        add(r, 0, from_left(sums.pop((r, tiles))))
        add(r, tiles - 1, from_right(sums.pop((r, -1))))
        for t in range(tiles):
            emit(r, t, sums.pop((r, t)))

    for r in range(rows):
        for t in (*range(1, tiles - 1), 0, tiles - 1):
            kept, flows = amounts_at(r, t)
            if kept is not None:
                add(r, t, kept)
            for flow, (dr, dc) in zip(flows, OFFSETS):
                add(r + dr, t + dc, flow)
        if r == rows - 1:
            for t in range(-1, tiles + 1):
                add(0, t, from_above(sums.pop((rows, t))))
        if r == 0:
            for t in range(-1, tiles + 1):
                add(rows - 1, t, from_below(sums.pop((-1, t))))
        if r >= 2:
            finish(r - 1)
    finish(rows - 1)
    finish(0)


def picked(bits, values):
    for bit in bits:
        values = [jnp.where(bit, odd, even) for even, odd in zip(values[0::2], values[1::2])]
    return values[0]


class Level:
    def __init__(self, first, rows, tiles, rate, parts, bits, weight):
        self.first, self.rows, self.tiles = first, rows, tiles
        self.rate, self.parts, self.bits, self.weight = rate, parts, bits, weight

    def at(self, r, t):
        return r * self.tiles + t

    def cells(self):
        return [(r, t) for r in range(self.rows) for t in range(self.tiles)]

    def line(self, r):
        return pl.ds(self.first + r, 8, stride=self.rows)

    def get(self, ref, r, t):
        return ref[t, self.line(r), :]

    def put(self, ref, r, t, value):
        ref[t, self.line(r), :] = value

    def fill(self, rate_at, code_at, opening_at):
        opening = {}

        def amounts_at(r, t):
            rate, code = rate_at(r, t), code_at(r, t)
            opening[r, t] = opening_at(r, t)
            for side, column_step, lane in ((0, -1, 0), (self.tiles - 1, 1, LANES - 1)):
                if t == side:
                    for d, (_, dc) in enumerate(OFFSETS):
                        if dc == column_step:
                            code = jnp.where(code == jnp.where(lane_ids() == lane, float(d), -1.0), 8.0, code)
                    rate = jnp.where(code == 8.0, 0.0, rate)
            masks = [code == float(d) for d in range(8)]
            self.put(self.rate, r, t, rate)
            for d, mask in enumerate(masks):
                self.put(self.parts.at[d], r, t, jnp.where(mask, rate, 0.0))
            number = code.astype(jnp.int32)
            for n in range(3):
                self.put(self.bits.at[n], r, t, number & (1 << n))
            return None, [jnp.where(mask, opening[r, t], 0.0) for mask in masks]

        def emit(r, t, count):
            self.put(self.weight, r, t, opening[r, t] / jnp.maximum(count, 1.0))

        sweep(self.rows, self.tiles, amounts_at, emit)

    def advance(self, rho, base=0):
        rows, tiles = self.rows, self.tiles
        field, room = {}, {}

        def load(r):
            for t in range(tiles):
                field[r, t] = rho[base + self.at(r, t)]
                room[r, t] = (1.0 - field[r, t]) * self.get(self.weight, r, t)
            room[r, -1] = from_left(room[r, tiles - 1])
            room[r, tiles] = from_right(room[r, 0])

        def amounts_at(r, t):
            needed = [row for row in (r - 1, r, r + 1) if 0 <= row < rows] + [rows - 1] * (r == 0)
            for row in needed:
                if (row, 0) not in room:
                    load(row)
            if r == 0 and (-1, 0) not in room:
                for tt in range(-1, tiles + 1):
                    room[-1, tt] = from_above(room[rows - 1, tt])
            if r == rows - 1 and (rows, 0) not in room:
                for tt in range(-1, tiles + 1):
                    room[rows, tt] = from_below(room[0, tt])
            bits = [self.get(self.bits.at[n], r, t) != 0 for n in range(3)]
            leaving = picked(bits, [room[r + dr, t + dc] for dr, dc in OFFSETS])
            share = field[r, t] * leaving
            flows = [self.get(self.parts.at[d], r, t) * share for d in range(8)]
            return field[r, t] - self.get(self.rate, r, t) * share, flows

        def emit(r, t, value):
            rho[base + self.at(r, t)] = value

        sweep(rows, tiles, amounts_at, emit)


def halved(coarse, lines, change=lambda tile: tile):
    def at(r, t):
        upper, lower = (pl.ds(2 * (coarse.first + r) + i, 8, stride=2 * coarse.rows) for i in range(2))
        a, b, c, d = (
            change(lines[2 * t + j, rows, :]) for j, rows in ((0, upper), (0, lower), (1, upper), (1, lower))
        )
        return 0.25 * (((a + b) + c) + d)

    return {(r, t): at(r, t) for r, t in coarse.cells()}


def is_open(value):
    return jnp.where(value > 0.0, 1.0, 0.0)


def main_kernel(
    own, crossed, paired, out, rate, code, start, sending, parts, bits, weight, rho,
    crate, cparts, cbits, cweight, pair, last_guess, result, sems,
):
    even = lax.axis_index("strip") % 2 == 0
    fields = (rate, code, start)
    for i, field in enumerate(fields):
        for t in range(TILES):
            for block in range(HEIGHT // 8):
                field[t, pl.ds(MARGIN + 8 * block, 8), :] = own[t, pl.ds(HEIGHT * i + 8 * block, 8), :]

    zeros = jnp.zeros((8, LANES), jnp.float32)

    def place_halo(tiles_at, high):
        place = pl.multiple_of(jnp.where(high, MARGIN + HEIGHT, MARGIN - HALO), 8)
        beyond = pl.ds(pl.multiple_of(jnp.where(high, SPAN - 8, 0), 8), 8)
        for i, field in enumerate(fields):
            for block in range(HALO // 8):
                for t, tile in enumerate(tiles_at(HALO * i + 8 * block)):
                    field[t, pl.ds(place + 8 * block, 8), :] = tile
        s = sublane_ids()
        for t, tile in enumerate(tiles_at(3 * HALO)):
            there = jnp.where(high, s, 7 - s) < 2
            turned = jnp.where(high, pltpu.roll(tile, 6, 0), pltpu.roll(tile, 2, 0))
            rate[t, beyond, :] = jnp.where(there, tile, 0.0)
            code[t, beyond, :] = jnp.where(there, turned, 0.0)
            start[t, beyond, :] = zeros

    place_halo(lambda row: [paired[t, pl.ds(row, 8), :] for t in range(TILES)], even)
    place_halo(
        lambda row: interleave([crossed[t, pl.ds(row, 8), :] for t in range(TILES)]), jnp.logical_not(even)
    )
    for field in fields:
        for t in range(TILES):
            field[t, pl.ds(SPAN, 8), :] = zeros

    stages = [
        (Level(*window, TILES, sending, parts, bits, weight), Level(*window_c, TILES_C, crate, cparts, cbits, cweight))
        for window, window_c in zip(STAGES, STAGES_C)
    ]
    fine, coarse = stages[0]
    openings = {}

    def rate_at(r, t):
        value = fine.get(rate, r, t)
        openings[r, t] = is_open(value)
        return value

    fine.fill(rate_at, lambda r, t: fine.get(code, r, t), lambda r, t: openings[r, t])
    mean_rate = halved(coarse, rate)
    mean_open = halved(coarse, rate, is_open)
    def coarse_code_at(r, t):
        return code[2 * t, pl.ds(2 * (coarse.first + r), 8, stride=2 * coarse.rows), :]

    coarse.fill(lambda r, t: mean_rate[r, t], coarse_code_at, lambda r, t: mean_open[r, t])

    n = lax.axis_index("tm")

    half = SPAN_C * TILES_C // 8

    @pl.when(n > 0)
    def _():
        for (r, t), value in halved(coarse, start).items():
            pair[coarse.at(r, t)] = value

        @pl.loop(0, CSTEPS)
        def _(step):
            coarse.advance(pair)

        for r, t in coarse.cells():
            coarse.put(last_guess, r, t, pair[coarse.at(r, t)])

    for r, t in fine.cells():
        rho[fine.at(r, t)] = fine.get(start, r, t)

    @pl.loop(0, FINE)
    def _(step):
        fine.advance(rho)

    for r, t in fine.cells():
        fine.put(start, r, t, rho[fine.at(r, t)])

    def stage(m):
        fine, coarse = stages[m]

        @pl.when(n >= m)
        def _():
            for (r, t), value in halved(coarse, start).items():
                pair[half + coarse.at(r, t)] = value
            for r, t in coarse.cells():
                value = coarse.get(last_guess, r, t)
                pair[coarse.at(r, t)] = value
                for i in range(4):
                    rho[fine.at(2 * r + i // 2, 2 * t + i % 2)] = value

            @pl.loop(0, FINE)
            def _(step):
                fine.advance(rho)

            @pl.loop(0, CSTEPS)
            def _(step):
                coarse.advance(pair)
                coarse.advance(pair, half)

            for r, t in coarse.cells():
                value = pair[coarse.at(r, t)]
                change = pair[half + coarse.at(r, t)] - value
                coarse.put(last_guess, r, t, value)
                for i in range(4):
                    rr, tt = 2 * r + i // 2, 2 * t + i % 2
                    fine.put(start, rr, tt, rho[fine.at(rr, tt)] + change)

    for m in range(1, len(STAGES)):
        stage(m)

    copies = []
    for block in range(HEIGHT // 8):
        rows = pl.ds(MARGIN + 8 * block, 8)
        for j, value in enumerate(deinterleave([start[t, rows, :] for t in range(TILES)])):
            result[pl.ds(8 * block, 8), pl.ds(LANES * j, LANES)] = value
        if block % 2:
            rows = pl.ds(8 * (block - 1), 16)
            copies.append(pltpu.make_async_copy(result.at[rows, :], out.at[rows, :], sems.at[block // 2]))
            copies[-1].start()
    for item in copies:
        item.wait()


def per_device(density, speed, codes, obstacle):
    f32, i32 = jnp.float32, jnp.int32
    args = (density, speed, codes, obstacle)
    sent_shape = pltpu.VMEM((TILES, SENT, LANES), f32)
    to_cross = pl.pallas_call(
        cross_kernel,
        out_shape=sent_shape,
        in_specs=[pl.BlockSpec(memory_space=pl.ANY)] * 4,
        scratch_shapes=[pltpu.VMEM((40, TILES * LANES), x.dtype) for x in args] + [pltpu.SemaphoreType.DMA((4,))],
        name="cross",
    )(*args)
    count = lax.axis_size("strip")
    across = [(i, i + 1) for i in range(1, count - 1, 2)]
    within = [(i, i + 1) for i in range(0, count, 2)]
    crossed = lax.ppermute(to_cross, "strip", across + [(j, i) for i, j in across])
    own, to_pair = pl.pallas_call(
        own_kernel,
        out_shape=(pltpu.VMEM((TILES, 3 * HEIGHT, LANES), f32), sent_shape),
        cost_estimate=pl.CostEstimate(flops=10_000_000, bytes_accessed=2_000_000, transcendentals=0),
        name="own",
    )(*args)
    paired = lax.ppermute(to_pair, "strip", within + [(j, i) for i, j in within])

    fine_lines = (TILES, SPAN + 8, LANES)
    coarse_lines = (TILES_C, SPAN_C, LANES)
    result = pl.pallas_call(
        main_kernel,
        out_shape=jax.ShapeDtypeStruct((HEIGHT, TILES * LANES), f32),
        in_specs=[pl.BlockSpec(memory_space=pltpu.VMEM)] * 3,
        scratch_shapes=[
            pltpu.VMEM(fine_lines, f32),
            pltpu.VMEM(fine_lines, f32),
            pltpu.VMEM(fine_lines, f32),
            pltpu.VMEM(fine_lines, f32),
            pltpu.VMEM((8, *fine_lines), f32),
            pltpu.VMEM((3, *fine_lines), i32),
            pltpu.VMEM(fine_lines, f32),
            pltpu.VMEM((STAGES[0][1] * TILES, 8, LANES), f32),
            pltpu.VMEM(coarse_lines, f32),
            pltpu.VMEM((8, *coarse_lines), f32),
            pltpu.VMEM((3, *coarse_lines), i32),
            pltpu.VMEM(coarse_lines, f32),
            pltpu.VMEM((2 * SPAN_C * TILES_C // 8, 8, LANES), f32),
            pltpu.VMEM(coarse_lines, f32),
            pltpu.VMEM((HEIGHT, TILES * LANES), f32),
            pltpu.SemaphoreType.DMA((4,)),
        ],
        out_specs=pl.BlockSpec(memory_space=pl.ANY),
        compiler_params=pltpu.CompilerParams(vmem_limit_bytes=32 * 1024 * 1024),
        name="parareal",
    )(own, crossed, paired)
    return result[None]


def solution(mesh):
    in_specs = (P("strip", None), P("strip", None), P("strip", None), P("strip", None))
    out_specs = P("tm", "strip", None)
    return jax.shard_map(
        per_device, mesh=mesh, in_specs=in_specs, out_specs=out_specs, check_vma=False
    )
```

```python
import jax
import jax.numpy as jnp
from jax import lax
from jax.experimental import pallas as pl
from jax.experimental.pallas import tpu as pltpu
from jax.sharding import PartitionSpec as P

FINE = 8
CSTEPS = 4
LAMBDA = 0.9
OFFSETS = ((0, 1), (-1, 1), (-1, 0), (-1, -1), (0, -1), (1, -1), (1, 0), (1, 1))

LANES = 128
TILES = 4
TILES_C = TILES // 2
HEIGHT = 64
HALO = 32
MARGIN = 40
SPAN = HEIGHT + 2 * MARGIN
SENT = 3 * HALO + 8
STAGES = ((7, 17), (16, 14), (24, 12), (32, 10))
STAGES_C = ((3, 9), (8, 7), (12, 6), (16, 5))
SPAN_C = (SPAN + 8) // 2


def lane_ids():
    return lax.broadcasted_iota(jnp.int32, (8, LANES), 1)


def sublane_ids():
    return lax.broadcasted_iota(jnp.int32, (8, LANES), 0)


def interleave(tiles):
    lane = lane_ids()
    result = []
    for t in range(TILES):
        index = (lane * TILES + t) % LANES
        picked = [jnp.take_along_axis(tile, index, axis=1) for tile in tiles]
        merged = picked[3]
        for j in (2, 1, 0):
            merged = jnp.where(lane < 32 * (j + 1), picked[j], merged)
        result.append(merged)
    return result


def deinterleave(tiles):
    lane = lane_ids()
    part = lane % TILES
    result = []
    for j in range(TILES):
        index = lane // TILES + 32 * j
        picked = [jnp.take_along_axis(tile, index, axis=1) for tile in tiles]
        merged = picked[3]
        for t in (2, 1, 0):
            merged = jnp.where(part == t, picked[t], merged)
        result.append(merged)
    return result


def products(density, speed, codes, obstacle, rows):
    cols = [pl.ds(LANES * j, LANES) for j in range(TILES)]
    opening = [1.0 - obstacle[rows, c].astype(jnp.float32) for c in cols]
    rate = [LAMBDA * speed[rows, c] * o for c, o in zip(cols, opening)]
    start = [density[rows, c] * o for c, o in zip(cols, opening)]
    code = [codes[rows, c].astype(jnp.float32) for c in cols]
    return rate, code, start


def edge_tile(rate, code, to_next):
    s = sublane_ids()
    below = jnp.where(s >= 6, rate, pltpu.roll(code, 6, 0))
    above = jnp.where(s < 2, rate, pltpu.roll(code, 2, 0))
    return jnp.where(to_next, below, above)


def cross_kernel(density, speed, codes, obstacle, sent, d_buf, s_buf, c_buf, o_buf, sems):
    odd = lax.axis_index("strip") % 2
    rows = pl.ds(pl.multiple_of(24 * odd, 8), 40)
    bufs = (d_buf, s_buf, c_buf, o_buf)
    copies = [
        pltpu.make_async_copy(source.at[rows, :], buf, sems.at[i])
        for i, (source, buf) in enumerate(zip((density, speed, codes, obstacle), bufs))
    ]
    for item in copies:
        item.start()
    for item in copies:
        item.wait()
    for block in range(4):
        fields = products(*bufs, pl.ds(pl.multiple_of(8 * (block + odd), 8), 8))
        for field, tiles in enumerate(fields):
            for t, value in enumerate(tiles):
                sent[t, pl.ds(HALO * field + 8 * block, 8), :] = value
    rate, code, _ = products(*bufs, pl.ds(pl.multiple_of(32 * (1 - odd), 8), 8))
    for t in range(TILES):
        sent[t, pl.ds(3 * HALO, 8), :] = edge_tile(rate[t], code[t], odd == 1)


def own_kernel(density, speed, codes, obstacle, own, sent):
    even = lax.axis_index("strip") % 2 == 0
    for block in range(HEIGHT // 8):
        fields = products(density, speed, codes, obstacle, pl.ds(8 * block, 8))
        for field, tiles in enumerate(fields):
            for t, value in enumerate(interleave(tiles)):
                own[t, pl.ds(HEIGHT * field + 8 * block, 8), :] = value
    for t in range(TILES):
        for field in range(3):
            for block in range(4):
                first, second = (own[t, pl.ds(HEIGHT * field + 8 * b, 8), :] for b in (block, block + 4))
                sent[t, pl.ds(HALO * field + 8 * block, 8), :] = jnp.where(even, second, first)
        rate, code = (
            jnp.where(even, own[t, pl.ds(HEIGHT * field + 24, 8), :], own[t, pl.ds(HEIGHT * field + 32, 8), :])
            for field in range(2)
        )
        sent[t, pl.ds(3 * HALO, 8), :] = edge_tile(rate, code, even)


def from_left(tile):
    return pltpu.roll(tile, 1, 1)


def from_right(tile):
    return pltpu.roll(tile, LANES - 1, 1)


def from_above(tile):
    return jnp.where(sublane_ids() == 0, 0.0, pltpu.roll(tile, 1, 0))


def from_below(tile):
    return jnp.where(sublane_ids() == 7, 0.0, pltpu.roll(tile, 7, 0))


def sweep(rows, tiles, amounts_at, emit):
    sums = {}

    def add(r, t, value):
        sums[r, t] = sums[r, t] + value if (r, t) in sums else value

    def finish(r):
        add(r, 0, from_left(sums.pop((r, tiles))))
        add(r, tiles - 1, from_right(sums.pop((r, -1))))
        for t in range(tiles):
            emit(r, t, sums.pop((r, t)))

    for r in range(rows):
        for t in (*range(1, tiles - 1), 0, tiles - 1):
            kept, flows = amounts_at(r, t)
            if kept is not None:
                add(r, t, kept)
            for flow, (dr, dc) in zip(flows, OFFSETS):
                add(r + dr, t + dc, flow)
        if r == rows - 1:
            for t in range(-1, tiles + 1):
                add(0, t, from_above(sums.pop((rows, t))))
        if r == 0:
            for t in range(-1, tiles + 1):
                add(rows - 1, t, from_below(sums.pop((-1, t))))
        if r >= 2:
            finish(r - 1)
    finish(rows - 1)
    finish(0)


def picked(bits, values):
    for bit in bits:
        values = [jnp.where(bit, odd, even) for even, odd in zip(values[0::2], values[1::2])]
    return values[0]


SIDES = [[d for d, (_, dc) in enumerate(OFFSETS) if dc == step] for step in (1, -1)]


class Level:
    def __init__(self, first, rows, tiles, rate, parts, bits, weight, sides=None):
        self.first, self.rows, self.tiles, self.sides = first, rows, tiles, sides
        self.rate, self.parts, self.bits, self.weight = rate, parts, bits, weight

    def at(self, r, t):
        return r * self.tiles + t

    def cells(self):
        return [(r, t) for r in range(self.rows) for t in range(self.tiles)]

    def line(self, r):
        return pl.ds(self.first + r, 8, stride=self.rows)

    def get(self, ref, r, t):
        return ref[t, self.line(r), :]

    def put(self, ref, r, t, value):
        ref[t, self.line(r), :] = value

    def fill(self, rate_at, code_at, opening_at):
        opening = {}

        def amounts_at(r, t):
            rate, code = rate_at(r, t), code_at(r, t)
            opening[r, t] = opening_at(r, t)
            for side, column_step, lane in ((0, -1, 0), (self.tiles - 1, 1, LANES - 1)):
                if t == side:
                    for d, (_, dc) in enumerate(OFFSETS):
                        if dc == column_step:
                            code = jnp.where(code == jnp.where(lane_ids() == lane, float(d), -1.0), 8.0, code)
                    rate = jnp.where(code == 8.0, 0.0, rate)
            masks = [code == float(d) for d in range(8)]
            self.put(self.rate, r, t, rate)
            for d, mask in enumerate(masks):
                part = jnp.where(mask, rate, 0.0)
                self.put(self.parts.at[d], r, t, part)
                if self.sides is None:
                    continue
                if t == self.tiles - 1 and d in SIDES[0]:
                    self.sides[SIDES[0].index(d), self.line(r), :] = from_left(part)
                if t == 0 and d in SIDES[1]:
                    self.sides[3 + SIDES[1].index(d), self.line(r), :] = from_right(part)
            number = code.astype(jnp.int32)
            for n in range(3):
                self.put(self.bits.at[n], r, t, number & (1 << n))
            return None, [jnp.where(mask, opening[r, t], 0.0) for mask in masks]

        def emit(r, t, count):
            self.put(self.weight, r, t, opening[r, t] / jnp.maximum(count, 1.0))

        sweep(self.rows, self.tiles, amounts_at, emit)

    def advance(self, rho, base=0):
        (self.advance_rolling_sums if self.sides is None else self.advance_entering)(rho, base)

    def advance_rolling_sums(self, rho, base):
        rows, tiles = self.rows, self.tiles
        field, room = {}, {}

        def load(r):
            for t in range(tiles):
                field[r, t] = rho[base + self.at(r, t)]
                room[r, t] = (1.0 - field[r, t]) * self.get(self.weight, r, t)
            room[r, -1] = from_left(room[r, tiles - 1])
            room[r, tiles] = from_right(room[r, 0])

        def amounts_at(r, t):
            needed = [row for row in (r - 1, r, r + 1) if 0 <= row < rows] + [rows - 1] * (r == 0)
            for row in needed:
                if (row, 0) not in room:
                    load(row)
            if r == 0 and (-1, 0) not in room:
                for tt in range(-1, tiles + 1):
                    room[-1, tt] = from_above(room[rows - 1, tt])
            if r == rows - 1 and (rows, 0) not in room:
                for tt in range(-1, tiles + 1):
                    room[rows, tt] = from_below(room[0, tt])
            bits = [self.get(self.bits.at[n], r, t) != 0 for n in range(3)]
            leaving = picked(bits, [room[r + dr, t + dc] for dr, dc in OFFSETS])
            share = field[r, t] * leaving
            flows = [self.get(self.parts.at[d], r, t) * share for d in range(8)]
            return field[r, t] - self.get(self.rate, r, t) * share, flows

        def emit(r, t, value):
            rho[base + self.at(r, t)] = value

        sweep(rows, tiles, amounts_at, emit)

    def advance_entering(self, rho, base):
        rows, tiles = self.rows, self.tiles
        field, room, sums, entering = {}, {}, {}, {}

        def load(r):
            for t in range(tiles):
                field[r, t] = rho[base + self.at(r, t)]
                room[r, t] = (1.0 - field[r, t]) * self.get(self.weight, r, t)
            field[r, -1] = from_left(field[r, tiles - 1])
            field[r, tiles] = from_right(field[r, 0])
            room[r, -1] = from_left(room[r, tiles - 1])
            room[r, tiles] = from_right(room[r, 0])

        def add(target, key, value):
            target[key] = target[key] + value if key in target else value

        def finish(r):
            add(sums, (r, 0), room[r, 0] * entering.pop((r, 0)))
            add(sums, (r, tiles - 1), room[r, tiles - 1] * entering.pop((r, 1)))
            for t in range(tiles):
                rho[base + self.at(r, t)] = sums.pop((r, t))

        for r in range(rows):
            needed = [row for row in (r - 1, r, r + 1) if 0 <= row < rows] + [rows - 1] * (r == 0)
            for row in needed:
                if (row, 0) not in room:
                    load(row)
            if r == 0:
                for t in range(-1, tiles + 1):
                    room[-1, t] = from_above(room[rows - 1, t])
            if r == rows - 1:
                for t in range(-1, tiles + 1):
                    room[rows, t] = from_below(room[0, t])
            for t in (*range(1, tiles - 1), 0, tiles - 1):
                bits = [self.get(self.bits.at[n], r, t) != 0 for n in range(3)]
                leaving = picked(bits, [room[r + dr, t + dc] for dr, dc in OFFSETS])
                share = field[r, t] * leaving
                add(sums, (r, t), field[r, t] - self.get(self.rate, r, t) * share)
                for d, (dr, dc) in enumerate(OFFSETS):
                    if 0 <= t + dc < tiles:
                        add(sums, (r + dr, t + dc), self.get(self.parts.at[d], r, t) * share)
            for side, directions in enumerate(SIDES):
                for i, d in enumerate(directions):
                    pushed = self.sides[3 * side + i, self.line(r), :] * field[r, (-1, tiles)[side]]
                    add(entering, (r + OFFSETS[d][0], side), pushed)
            for row, target, moved in ((rows - 1, 0, from_above), (0, rows - 1, from_below)):
                if r == row:
                    beyond = rows if row else -1
                    for t in range(tiles):
                        add(sums, (target, t), moved(sums.pop((beyond, t))))
                    for side in range(2):
                        add(entering, (target, side), moved(entering.pop((beyond, side))))
            if r >= 2:
                finish(r - 1)
        finish(rows - 1)
        finish(0)


def halved(coarse, lines, change=lambda tile: tile):
    def at(r, t):
        upper, lower = (pl.ds(2 * (coarse.first + r) + i, 8, stride=2 * coarse.rows) for i in range(2))
        a, b, c, d = (
            change(lines[2 * t + j, rows, :]) for j, rows in ((0, upper), (0, lower), (1, upper), (1, lower))
        )
        return 0.25 * (((a + b) + c) + d)

    return {(r, t): at(r, t) for r, t in coarse.cells()}


def is_open(value):
    return jnp.where(value > 0.0, 1.0, 0.0)


def main_kernel(
    own, crossed, paired, out, rate, code, start, sending, parts, bits, weight, rho,
    crate, cparts, cbits, cweight, csides, pair, last_guess, result, sems,
):
    even = lax.axis_index("strip") % 2 == 0
    fields = (rate, code, start)
    for i, field in enumerate(fields):
        for t in range(TILES):
            for block in range(HEIGHT // 8):
                field[t, pl.ds(MARGIN + 8 * block, 8), :] = own[t, pl.ds(HEIGHT * i + 8 * block, 8), :]

    zeros = jnp.zeros((8, LANES), jnp.float32)

    def place_halo(tiles_at, high):
        place = pl.multiple_of(jnp.where(high, MARGIN + HEIGHT, MARGIN - HALO), 8)
        beyond = pl.ds(pl.multiple_of(jnp.where(high, SPAN - 8, 0), 8), 8)
        for i, field in enumerate(fields):
            for block in range(HALO // 8):
                for t, tile in enumerate(tiles_at(HALO * i + 8 * block)):
                    field[t, pl.ds(place + 8 * block, 8), :] = tile
        s = sublane_ids()
        for t, tile in enumerate(tiles_at(3 * HALO)):
            there = jnp.where(high, s, 7 - s) < 2
            turned = jnp.where(high, pltpu.roll(tile, 6, 0), pltpu.roll(tile, 2, 0))
            rate[t, beyond, :] = jnp.where(there, tile, 0.0)
            code[t, beyond, :] = jnp.where(there, turned, 0.0)
            start[t, beyond, :] = zeros

    place_halo(lambda row: [paired[t, pl.ds(row, 8), :] for t in range(TILES)], even)
    place_halo(
        lambda row: interleave([crossed[t, pl.ds(row, 8), :] for t in range(TILES)]), jnp.logical_not(even)
    )
    for field in fields:
        for t in range(TILES):
            field[t, pl.ds(SPAN, 8), :] = zeros

    stages = [
        (
            Level(*window, TILES, sending, parts, bits, weight),
            Level(*window_c, TILES_C, crate, cparts, cbits, cweight, csides),
        )
        for window, window_c in zip(STAGES, STAGES_C)
    ]
    fine, coarse = stages[0]
    openings = {}

    def rate_at(r, t):
        value = fine.get(rate, r, t)
        openings[r, t] = is_open(value)
        return value

    fine.fill(rate_at, lambda r, t: fine.get(code, r, t), lambda r, t: openings[r, t])
    mean_rate = halved(coarse, rate)
    mean_open = halved(coarse, rate, is_open)
    def coarse_code_at(r, t):
        return code[2 * t, pl.ds(2 * (coarse.first + r), 8, stride=2 * coarse.rows), :]

    coarse.fill(lambda r, t: mean_rate[r, t], coarse_code_at, lambda r, t: mean_open[r, t])

    n = lax.axis_index("tm")

    half = SPAN_C * TILES_C // 8

    for (r, t), value in halved(coarse, start).items():
        pair[coarse.at(r, t)] = value
    for r, t in fine.cells():
        rho[fine.at(r, t)] = fine.get(start, r, t)

    @pl.loop(0, CSTEPS)
    def _(step):
        fine.advance(rho)
        coarse.advance(pair)

    @pl.loop(CSTEPS, FINE)
    def _(step):
        fine.advance(rho)

    for r, t in coarse.cells():
        coarse.put(last_guess, r, t, pair[coarse.at(r, t)])
    for r, t in fine.cells():
        fine.put(start, r, t, rho[fine.at(r, t)])

    def stage(m):
        fine, coarse = stages[m]

        @pl.when(n >= m)
        def _():
            for (r, t), value in halved(coarse, start).items():
                pair[half + coarse.at(r, t)] = value
            for r, t in coarse.cells():
                value = coarse.get(last_guess, r, t)
                pair[coarse.at(r, t)] = value
                for i in range(4):
                    rho[fine.at(2 * r + i // 2, 2 * t + i % 2)] = value

            @pl.loop(0, FINE)
            def _(step):
                fine.advance(rho)
                coarse.advance(pair, half * (step // CSTEPS))

            for r, t in coarse.cells():
                value = pair[coarse.at(r, t)]
                change = pair[half + coarse.at(r, t)] - value
                coarse.put(last_guess, r, t, value)
                for i in range(4):
                    rr, tt = 2 * r + i // 2, 2 * t + i % 2
                    fine.put(start, rr, tt, rho[fine.at(rr, tt)] + change)

    for m in range(1, len(STAGES)):
        stage(m)

    copies = []
    for block in range(HEIGHT // 8):
        rows = pl.ds(MARGIN + 8 * block, 8)
        for j, value in enumerate(deinterleave([start[t, rows, :] for t in range(TILES)])):
            result[pl.ds(8 * block, 8), pl.ds(LANES * j, LANES)] = value
        if block % 2:
            rows = pl.ds(8 * (block - 1), 16)
            copies.append(pltpu.make_async_copy(result.at[rows, :], out.at[rows, :], sems.at[block // 2]))
            copies[-1].start()
    for item in copies:
        item.wait()


def per_device(density, speed, codes, obstacle):
    f32, i32 = jnp.float32, jnp.int32
    args = (density, speed, codes, obstacle)
    sent_shape = pltpu.VMEM((TILES, SENT, LANES), f32)
    to_cross = pl.pallas_call(
        cross_kernel,
        out_shape=sent_shape,
        in_specs=[pl.BlockSpec(memory_space=pl.ANY)] * 4,
        scratch_shapes=[pltpu.VMEM((40, TILES * LANES), x.dtype) for x in args] + [pltpu.SemaphoreType.DMA((4,))],
        name="cross",
    )(*args)
    count = lax.axis_size("strip")
    across = [(i, i + 1) for i in range(1, count - 1, 2)]
    within = [(i, i + 1) for i in range(0, count, 2)]
    crossed = lax.ppermute(to_cross, "strip", across + [(j, i) for i, j in across])
    own, to_pair = pl.pallas_call(
        own_kernel,
        out_shape=(pltpu.VMEM((TILES, 3 * HEIGHT, LANES), f32), sent_shape),
        cost_estimate=pl.CostEstimate(flops=10_000_000, bytes_accessed=2_000_000, transcendentals=0),
        name="own",
    )(*args)
    paired = lax.ppermute(to_pair, "strip", within + [(j, i) for i, j in within])

    fine_lines = (TILES, SPAN + 8, LANES)
    coarse_lines = (TILES_C, SPAN_C, LANES)
    result = pl.pallas_call(
        main_kernel,
        out_shape=jax.ShapeDtypeStruct((HEIGHT, TILES * LANES), f32),
        in_specs=[pl.BlockSpec(memory_space=pltpu.VMEM)] * 3,
        scratch_shapes=[
            pltpu.VMEM(fine_lines, f32),
            pltpu.VMEM(fine_lines, f32),
            pltpu.VMEM(fine_lines, f32),
            pltpu.VMEM(fine_lines, f32),
            pltpu.VMEM((8, *fine_lines), f32),
            pltpu.VMEM((3, *fine_lines), i32),
            pltpu.VMEM(fine_lines, f32),
            pltpu.VMEM((STAGES[0][1] * TILES, 8, LANES), f32),
            pltpu.VMEM(coarse_lines, f32),
            pltpu.VMEM((8, *coarse_lines), f32),
            pltpu.VMEM((3, *coarse_lines), i32),
            pltpu.VMEM(coarse_lines, f32),
            pltpu.VMEM((6, *coarse_lines[1:]), f32),
            pltpu.VMEM((2 * SPAN_C * TILES_C // 8, 8, LANES), f32),
            pltpu.VMEM(coarse_lines, f32),
            pltpu.VMEM((HEIGHT, TILES * LANES), f32),
            pltpu.SemaphoreType.DMA((4,)),
        ],
        out_specs=pl.BlockSpec(memory_space=pl.ANY),
        compiler_params=pltpu.CompilerParams(vmem_limit_bytes=32 * 1024 * 1024),
        name="parareal",
    )(own, crossed, paired)
    return result[None]


def solution(mesh):
    in_specs = (P("strip", None), P("strip", None), P("strip", None), P("strip", None))
    out_specs = P("tm", "strip", None)
    return jax.shard_map(
        per_device, mesh=mesh, in_specs=in_specs, out_specs=out_specs, check_vma=False
    )
```

```python
import jax
import jax.numpy as jnp
from jax import lax
from jax.experimental import pallas as pl
from jax.experimental.pallas import tpu as pltpu
from jax.sharding import PartitionSpec as P

FINE = 8
CSTEPS = 4
LAMBDA = 0.9
OFFSETS = ((0, 1), (-1, 1), (-1, 0), (-1, -1), (0, -1), (1, -1), (1, 0), (1, 1))

LANES = 128
TILES = 4
TILES_C = TILES // 2
HEIGHT = 64
HALO = 32
MARGIN = 40
SPAN = HEIGHT + 2 * MARGIN
SENT = 3 * HALO + 8
STAGES = ((7, 17), (16, 14), (24, 12), (32, 10))
STAGES_C = ((3, 9), (8, 7), (12, 6), (16, 5))
LINES, LINES_C = 168, 88


def lane_ids():
    return lax.broadcasted_iota(jnp.int32, (8, LANES), 1)


def sublane_ids():
    return lax.broadcasted_iota(jnp.int32, (8, LANES), 0)


def interleave(tiles):
    lane = lane_ids()
    result = []
    for t in range(TILES):
        index = (lane * TILES + t) % LANES
        picked = [jnp.take_along_axis(tile, index, axis=1) for tile in tiles]
        merged = picked[3]
        for j in (2, 1, 0):
            merged = jnp.where(lane < 32 * (j + 1), picked[j], merged)
        result.append(merged)
    return result


def deinterleave(tiles):
    lane = lane_ids()
    part = lane % TILES
    result = []
    for j in range(TILES):
        index = lane // TILES + 32 * j
        picked = [jnp.take_along_axis(tile, index, axis=1) for tile in tiles]
        merged = picked[3]
        for t in (2, 1, 0):
            merged = jnp.where(part == t, picked[t], merged)
        result.append(merged)
    return result


def products(density, speed, codes, obstacle, rows):
    cols = [pl.ds(LANES * j, LANES) for j in range(TILES)]
    opening = [1.0 - obstacle[rows, c].astype(jnp.float32) for c in cols]
    rate = [LAMBDA * speed[rows, c] * o for c, o in zip(cols, opening)]
    start = [density[rows, c] * o for c, o in zip(cols, opening)]
    code = [codes[rows, c].astype(jnp.float32) for c in cols]
    return rate, code, start


def edge_tile(rate, code, to_next):
    s = sublane_ids()
    below = jnp.where(s >= 6, rate, pltpu.roll(code, 6, 0))
    above = jnp.where(s < 2, rate, pltpu.roll(code, 2, 0))
    return jnp.where(to_next, below, above)


def cross_kernel(density, speed, codes, obstacle, sent, d_buf, s_buf, c_buf, o_buf, sems):
    odd = lax.axis_index("strip") % 2
    rows = pl.ds(pl.multiple_of(24 * odd, 8), 40)
    bufs = (d_buf, s_buf, c_buf, o_buf)
    copies = [
        pltpu.make_async_copy(source.at[rows, :], buf, sems.at[i])
        for i, (source, buf) in enumerate(zip((density, speed, codes, obstacle), bufs))
    ]
    for item in copies:
        item.start()
    for item in copies:
        item.wait()
    for block in range(4):
        fields = products(*bufs, pl.ds(pl.multiple_of(8 * (block + odd), 8), 8))
        for field, tiles in enumerate(fields):
            for t, value in enumerate(tiles):
                sent[t, pl.ds(HALO * field + 8 * block, 8), :] = value
    rate, code, _ = products(*bufs, pl.ds(pl.multiple_of(32 * (1 - odd), 8), 8))
    for t in range(TILES):
        sent[t, pl.ds(3 * HALO, 8), :] = edge_tile(rate[t], code[t], odd == 1)


def own_kernel(density, speed, codes, obstacle, own, sent):
    even = lax.axis_index("strip") % 2 == 0
    for block in range(HEIGHT // 8):
        fields = products(density, speed, codes, obstacle, pl.ds(8 * block, 8))
        for field, tiles in enumerate(fields):
            for t, value in enumerate(interleave(tiles)):
                own[t, pl.ds(HEIGHT * field + 8 * block, 8), :] = value
    for t in range(TILES):
        for field in range(3):
            for block in range(4):
                first, second = (own[t, pl.ds(HEIGHT * field + 8 * b, 8), :] for b in (block, block + 4))
                sent[t, pl.ds(HALO * field + 8 * block, 8), :] = jnp.where(even, second, first)
        rate, code = (
            jnp.where(even, own[t, pl.ds(HEIGHT * field + 24, 8), :], own[t, pl.ds(HEIGHT * field + 32, 8), :])
            for field in range(2)
        )
        sent[t, pl.ds(3 * HALO, 8), :] = edge_tile(rate, code, even)


def from_left(tile):
    return pltpu.roll(tile, 1, 1)


def from_right(tile):
    return pltpu.roll(tile, LANES - 1, 1)


def from_above(tile):
    return jnp.where(sublane_ids() == 0, 0.0, pltpu.roll(tile, 1, 0))


def from_below(tile):
    return jnp.where(sublane_ids() == 7, 0.0, pltpu.roll(tile, 7, 0))


def sweep(rows, tiles, amounts_at, emit):
    sums = {}

    def add(r, t, value):
        sums[r, t] = sums[r, t] + value if (r, t) in sums else value

    def finish(r):
        add(r, 0, from_left(sums.pop((r, tiles))))
        add(r, tiles - 1, from_right(sums.pop((r, -1))))
        for t in range(tiles):
            emit(r, t, sums.pop((r, t)))

    for r in range(rows):
        for t in (*range(1, tiles - 1), 0, tiles - 1):
            kept, flows = amounts_at(r, t)
            if kept is not None:
                add(r, t, kept)
            for flow, (dr, dc) in zip(flows, OFFSETS):
                add(r + dr, t + dc, flow)
        if r == rows - 1:
            for t in range(-1, tiles + 1):
                add(0, t, from_above(sums.pop((rows, t))))
        if r == 0:
            for t in range(-1, tiles + 1):
                add(rows - 1, t, from_below(sums.pop((-1, t))))
        if r >= 2:
            finish(r - 1)
    finish(rows - 1)
    finish(0)


def picked(bits, values):
    for bit in bits:
        values = [jnp.where(bit, odd, even) for even, odd in zip(values[0::2], values[1::2])]
    return values[0]


SIDES = [[d for d, (_, dc) in enumerate(OFFSETS) if dc == step] for step in (1, -1)]


class Level:
    def __init__(self, first, rows, tiles, rate, parts, bits, weight, sides=None):
        self.first, self.rows, self.tiles, self.sides = first, rows, tiles, sides
        self.rate, self.parts, self.bits, self.weight = rate, parts, bits, weight

    def at(self, r, t):
        return r * self.tiles + t

    def cells(self):
        return [(r, t) for r in range(self.rows) for t in range(self.tiles)]

    def line(self, r):
        return pl.ds(self.first + r, 8, stride=self.rows)

    def get(self, ref, r, t):
        return ref[t, self.line(r), :]

    def put(self, ref, r, t, value):
        ref[t, self.line(r), :] = value

    def fill(self, rate_at, code_at, opening_at):
        opening = {}

        def amounts_at(r, t):
            rate, code = rate_at(r, t), code_at(r, t)
            opening[r, t] = opening_at(r, t)
            for side, column_step, lane in ((0, -1, 0), (self.tiles - 1, 1, LANES - 1)):
                if t == side:
                    for d, (_, dc) in enumerate(OFFSETS):
                        if dc == column_step:
                            code = jnp.where(code == jnp.where(lane_ids() == lane, float(d), -1.0), 8.0, code)
                    rate = jnp.where(code == 8.0, 0.0, rate)
            masks = [code == float(d) for d in range(8)]
            self.put(self.rate, r, t, rate)
            for d, mask in enumerate(masks):
                part = jnp.where(mask, rate, 0.0)
                self.put(self.parts.at[d], r, t, part)
                if self.sides is None:
                    continue
                if t == self.tiles - 1 and d in SIDES[0]:
                    self.sides[SIDES[0].index(d), self.line(r), :] = from_left(part)
                if t == 0 and d in SIDES[1]:
                    self.sides[3 + SIDES[1].index(d), self.line(r), :] = from_right(part)
            number = code.astype(jnp.int32)
            for n in range(3):
                self.put(self.bits.at[n], r, t, number & (1 << n))
            return None, [jnp.where(mask, opening[r, t], 0.0) for mask in masks]

        def emit(r, t, count):
            self.put(self.weight, r, t, opening[r, t] / jnp.maximum(count, 1.0))

        sweep(self.rows, self.tiles, amounts_at, emit)

    def advance(self, rho, base=0):
        (self.advance_rolling_sums if self.sides is None else self.advance_entering)(rho, base)

    def advance_rolling_sums(self, rho, base):
        rows, tiles = self.rows, self.tiles
        field, room = {}, {}

        def load(r):
            for t in range(tiles):
                field[r, t] = rho[base + self.at(r, t)]
                room[r, t] = (1.0 - field[r, t]) * self.get(self.weight, r, t)
            room[r, -1] = from_left(room[r, tiles - 1])
            room[r, tiles] = from_right(room[r, 0])

        def amounts_at(r, t):
            needed = [row for row in (r - 1, r, r + 1) if 0 <= row < rows] + [rows - 1] * (r == 0)
            for row in needed:
                if (row, 0) not in room:
                    load(row)
            if r == 0 and (-1, 0) not in room:
                for tt in range(-1, tiles + 1):
                    room[-1, tt] = from_above(room[rows - 1, tt])
            if r == rows - 1 and (rows, 0) not in room:
                for tt in range(-1, tiles + 1):
                    room[rows, tt] = from_below(room[0, tt])
            bits = [self.get(self.bits.at[n], r, t) != 0 for n in range(3)]
            leaving = picked(bits, [room[r + dr, t + dc] for dr, dc in OFFSETS])
            share = field[r, t] * leaving
            flows = [self.get(self.parts.at[d], r, t) * share for d in range(8)]
            return field[r, t] - self.get(self.rate, r, t) * share, flows

        def emit(r, t, value):
            rho[base + self.at(r, t)] = value

        sweep(rows, tiles, amounts_at, emit)

    def advance_entering(self, rho, base):
        rows, tiles = self.rows, self.tiles
        field, room, sums, entering = {}, {}, {}, {}

        def load(r):
            for t in range(tiles):
                field[r, t] = rho[base + self.at(r, t)]
                room[r, t] = (1.0 - field[r, t]) * self.get(self.weight, r, t)
            field[r, -1] = from_left(field[r, tiles - 1])
            field[r, tiles] = from_right(field[r, 0])
            room[r, -1] = from_left(room[r, tiles - 1])
            room[r, tiles] = from_right(room[r, 0])

        def add(target, key, value):
            target[key] = target[key] + value if key in target else value

        def finish(r):
            add(sums, (r, 0), room[r, 0] * entering.pop((r, 0)))
            add(sums, (r, tiles - 1), room[r, tiles - 1] * entering.pop((r, 1)))
            for t in range(tiles):
                rho[base + self.at(r, t)] = sums.pop((r, t))

        for r in range(rows):
            needed = [row for row in (r - 1, r, r + 1) if 0 <= row < rows] + [rows - 1] * (r == 0)
            for row in needed:
                if (row, 0) not in room:
                    load(row)
            if r == 0:
                for t in range(-1, tiles + 1):
                    room[-1, t] = from_above(room[rows - 1, t])
            if r == rows - 1:
                for t in range(-1, tiles + 1):
                    room[rows, t] = from_below(room[0, t])
            for t in (*range(1, tiles - 1), 0, tiles - 1):
                bits = [self.get(self.bits.at[n], r, t) != 0 for n in range(3)]
                leaving = picked(bits, [room[r + dr, t + dc] for dr, dc in OFFSETS])
                share = field[r, t] * leaving
                add(sums, (r, t), field[r, t] - self.get(self.rate, r, t) * share)
                for d, (dr, dc) in enumerate(OFFSETS):
                    if 0 <= t + dc < tiles:
                        add(sums, (r + dr, t + dc), self.get(self.parts.at[d], r, t) * share)
            for side, directions in enumerate(SIDES):
                for i, d in enumerate(directions):
                    pushed = self.sides[3 * side + i, self.line(r), :] * field[r, (-1, tiles)[side]]
                    add(entering, (r + OFFSETS[d][0], side), pushed)
            for row, target, moved in ((rows - 1, 0, from_above), (0, rows - 1, from_below)):
                if r == row:
                    beyond = rows if row else -1
                    for t in range(tiles):
                        add(sums, (target, t), moved(sums.pop((beyond, t))))
                    for side in range(2):
                        add(entering, (target, side), moved(entering.pop((beyond, side))))
            if r >= 2:
                finish(r - 1)
        finish(rows - 1)
        finish(0)


def halved(coarse, lines, change=lambda tile: tile):
    def at(r, t):
        upper, lower = (pl.ds(2 * (coarse.first + r) + i, 8, stride=2 * coarse.rows) for i in range(2))
        a, b, c, d = (
            change(lines[2 * t + j, rows, :]) for j, rows in ((0, upper), (0, lower), (1, upper), (1, lower))
        )
        return 0.25 * (((a + b) + c) + d)

    return {(r, t): at(r, t) for r, t in coarse.cells()}


def is_open(value):
    return jnp.where(value > 0.0, 1.0, 0.0)


def main_kernel(
    own, crossed, paired, out, rate, code, start, sending, parts, bits, weight, rho,
    crate, cparts, cbits, cweight, csides, pair, last_guess, result, sems,
):
    even = lax.axis_index("strip") % 2 == 0
    fields = (rate, code, start)
    for i, field in enumerate(fields):
        for t in range(TILES):
            for block in range(HEIGHT // 8):
                field[t, pl.ds(MARGIN + 8 * block, 8), :] = own[t, pl.ds(HEIGHT * i + 8 * block, 8), :]

    zeros = jnp.zeros((8, LANES), jnp.float32)

    def place_halo(tiles_at, high):
        place = pl.multiple_of(jnp.where(high, MARGIN + HEIGHT, MARGIN - HALO), 8)
        beyond = pl.ds(pl.multiple_of(jnp.where(high, SPAN - 8, 0), 8), 8)
        for i, field in enumerate(fields):
            for block in range(HALO // 8):
                for t, tile in enumerate(tiles_at(HALO * i + 8 * block)):
                    field[t, pl.ds(place + 8 * block, 8), :] = tile
        s = sublane_ids()
        for t, tile in enumerate(tiles_at(3 * HALO)):
            there = jnp.where(high, s, 7 - s) < 2
            turned = jnp.where(high, pltpu.roll(tile, 6, 0), pltpu.roll(tile, 2, 0))
            rate[t, beyond, :] = jnp.where(there, tile, 0.0)
            code[t, beyond, :] = jnp.where(there, turned, 0.0)
            start[t, beyond, :] = zeros

    place_halo(lambda row: [paired[t, pl.ds(row, 8), :] for t in range(TILES)], even)
    place_halo(
        lambda row: interleave([crossed[t, pl.ds(row, 8), :] for t in range(TILES)]), jnp.logical_not(even)
    )
    for field in fields:
        for t in range(TILES):
            field[t, pl.ds(SPAN, 8), :] = zeros

    stages = [
        (
            Level(*window, TILES, sending, parts, bits, weight),
            Level(*window_c, TILES_C, crate, cparts, cbits, cweight, csides),
        )
        for window, window_c in zip(STAGES, STAGES_C)
    ]
    fine, coarse = stages[0]
    openings = {}

    def rate_at(r, t):
        value = fine.get(rate, r, t)
        openings[r, t] = is_open(value)
        return value

    fine.fill(rate_at, lambda r, t: fine.get(code, r, t), lambda r, t: openings[r, t])
    mean_rate = halved(coarse, rate)
    mean_open = halved(coarse, rate, is_open)
    def coarse_code_at(r, t):
        return code[2 * t, pl.ds(2 * (coarse.first + r), 8, stride=2 * coarse.rows), :]

    coarse.fill(lambda r, t: mean_rate[r, t], coarse_code_at, lambda r, t: mean_open[r, t])

    n = lax.axis_index("tm")

    half = STAGES_C[0][1] * TILES_C

    for (r, t), value in halved(coarse, start).items():
        pair[coarse.at(r, t)] = value
    for r, t in fine.cells():
        rho[fine.at(r, t)] = fine.get(start, r, t)

    @pl.loop(0, CSTEPS)
    def _(step):
        fine.advance(rho)
        coarse.advance(pair)

    @pl.loop(CSTEPS, FINE)
    def _(step):
        fine.advance(rho)

    for r, t in coarse.cells():
        coarse.put(last_guess, r, t, pair[coarse.at(r, t)])
    for r, t in fine.cells():
        fine.put(start, r, t, rho[fine.at(r, t)])

    def stage(m):
        fine, coarse = stages[m]

        @pl.when(n >= m)
        def _():
            for (r, t), value in halved(coarse, start).items():
                pair[half + coarse.at(r, t)] = value
            for r, t in coarse.cells():
                value = coarse.get(last_guess, r, t)
                pair[coarse.at(r, t)] = value
                for i in range(4):
                    rho[fine.at(2 * r + i // 2, 2 * t + i % 2)] = value

            @pl.loop(0, FINE)
            def _(step):
                fine.advance(rho)
                coarse.advance(pair, half * (step // CSTEPS))

            for r, t in coarse.cells():
                value = pair[coarse.at(r, t)]
                change = pair[half + coarse.at(r, t)] - value
                coarse.put(last_guess, r, t, value)
                for i in range(4):
                    rr, tt = 2 * r + i // 2, 2 * t + i % 2
                    fine.put(start, rr, tt, rho[fine.at(rr, tt)] + change)

    for m in range(1, len(STAGES)):
        stage(m)

    copies = []
    for block in range(HEIGHT // 8):
        rows = pl.ds(MARGIN + 8 * block, 8)
        for j, value in enumerate(deinterleave([start[t, rows, :] for t in range(TILES)])):
            result[pl.ds(8 * block, 8), pl.ds(LANES * j, LANES)] = value
        if block % 2:
            rows = pl.ds(8 * (block - 1), 16)
            copies.append(pltpu.make_async_copy(result.at[rows, :], out.at[rows, :], sems.at[block // 2]))
            copies[-1].start()
    for item in copies:
        item.wait()


def per_device(density, speed, codes, obstacle):
    f32, i32 = jnp.float32, jnp.int32
    args = (density, speed, codes, obstacle)
    sent_shape = pltpu.VMEM((TILES, SENT, LANES), f32)
    to_cross = pl.pallas_call(
        cross_kernel,
        out_shape=sent_shape,
        in_specs=[pl.BlockSpec(memory_space=pl.ANY)] * 4,
        scratch_shapes=[pltpu.VMEM((40, TILES * LANES), x.dtype) for x in args] + [pltpu.SemaphoreType.DMA((4,))],
        name="cross",
    )(*args)
    count = lax.axis_size("strip")
    across = [(i, i + 1) for i in range(1, count - 1, 2)]
    within = [(i, i + 1) for i in range(0, count, 2)]
    crossed = lax.ppermute(to_cross, "strip", across + [(j, i) for i, j in across])
    own, to_pair = pl.pallas_call(
        own_kernel,
        out_shape=(pltpu.VMEM((TILES, 3 * HEIGHT, LANES), f32), sent_shape),
        cost_estimate=pl.CostEstimate(flops=10_000_000, bytes_accessed=2_000_000, transcendentals=0),
        name="own",
    )(*args)
    paired = lax.ppermute(to_pair, "strip", within + [(j, i) for i, j in within])

    fine_lines = (TILES, LINES, LANES)
    coarse_lines = (TILES_C, LINES_C, LANES)
    result = pl.pallas_call(
        main_kernel,
        out_shape=jax.ShapeDtypeStruct((HEIGHT, TILES * LANES), f32),
        in_specs=[pl.BlockSpec(memory_space=pltpu.VMEM)] * 3,
        scratch_shapes=[
            pltpu.VMEM(fine_lines, f32),
            pltpu.VMEM(fine_lines, f32),
            pltpu.VMEM(fine_lines, f32),
            pltpu.VMEM(fine_lines, f32),
            pltpu.VMEM((8, *fine_lines), f32),
            pltpu.VMEM((3, *fine_lines), i32),
            pltpu.VMEM(fine_lines, f32),
            pltpu.VMEM((STAGES[0][1] * TILES, 8, LANES), f32),
            pltpu.VMEM(coarse_lines, f32),
            pltpu.VMEM((8, *coarse_lines), f32),
            pltpu.VMEM((3, *coarse_lines), i32),
            pltpu.VMEM(coarse_lines, f32),
            pltpu.VMEM((6, *coarse_lines[1:]), f32),
            pltpu.VMEM((2 * STAGES_C[0][1] * TILES_C, 8, LANES), f32),
            pltpu.VMEM(coarse_lines, f32),
            pltpu.VMEM((HEIGHT, TILES * LANES), f32),
            pltpu.SemaphoreType.DMA((4,)),
        ],
        out_specs=pl.BlockSpec(memory_space=pl.ANY),
        compiler_params=pltpu.CompilerParams(vmem_limit_bytes=32 * 1024 * 1024),
        name="parareal",
    )(own, crossed, paired)
    return result[None]


def solution(mesh):
    in_specs = (P("strip", None), P("strip", None), P("strip", None), P("strip", None))
    out_specs = P("tm", "strip", None)
    return jax.shard_map(
        per_device, mesh=mesh, in_specs=in_specs, out_specs=out_specs, check_vma=False
    )
```

```python
import jax
import jax.numpy as jnp
from jax import lax
from jax.experimental import pallas as pl
from jax.experimental.pallas import tpu as pltpu
from jax.sharding import PartitionSpec as P

FINE = 8
CSTEPS = 4
LAMBDA = 0.9
OFFSETS = ((0, 1), (-1, 1), (-1, 0), (-1, -1), (0, -1), (1, -1), (1, 0), (1, 1))

LANES = 128
TILES = 4
TILES_C = TILES // 2
HEIGHT = 64
HALO = 32
MARGIN = 40
SPAN = HEIGHT + 2 * MARGIN
SENT = 3 * HALO + 8
STAGES = ((7, 17), (16, 14), (24, 12), (32, 10))
STAGES_C = ((3, 9), (8, 7), (12, 6), (16, 5))
LINES, LINES_C = 168, 88


def lane_ids():
    return lax.broadcasted_iota(jnp.int32, (8, LANES), 1)


def sublane_ids():
    return lax.broadcasted_iota(jnp.int32, (8, LANES), 0)


def exchange_blocks(tiles):
    lane = lane_ids()

    def swap(first, second, width):
        low = lane % (2 * width) < width
        return (
            jnp.where(low, first, pltpu.roll(second, width, 1)),
            jnp.where(low, pltpu.roll(first, LANES - width, 1), second),
        )

    a, b, c, d = tiles
    (a, c), (b, d) = swap(a, c, 64), swap(b, d, 64)
    return [*swap(a, b, 32), *swap(c, d, 32)]


def interleave(tiles):
    lane = lane_ids()
    index = TILES * (lane % 32) + lane // 32
    return exchange_blocks([jnp.take_along_axis(tile, index, axis=1) for tile in tiles])


def deinterleave(tiles):
    lane = lane_ids()
    index = 32 * (lane % TILES) + lane // TILES
    return [jnp.take_along_axis(tile, index, axis=1) for tile in exchange_blocks(tiles)]


def products(density, speed, codes, obstacle, rows):
    cols = [pl.ds(LANES * j, LANES) for j in range(TILES)]
    opening = [1.0 - obstacle[rows, c].astype(jnp.float32) for c in cols]
    rate = [LAMBDA * speed[rows, c] * o for c, o in zip(cols, opening)]
    start = [density[rows, c] * o for c, o in zip(cols, opening)]
    code = [codes[rows, c].astype(jnp.float32) for c in cols]
    return rate, code, start


def edge_tile(rate, code, to_next):
    s = sublane_ids()
    below = jnp.where(s >= 6, rate, pltpu.roll(code, 6, 0))
    above = jnp.where(s < 2, rate, pltpu.roll(code, 2, 0))
    return jnp.where(to_next, below, above)


def cross_kernel(density, speed, codes, obstacle, sent, d_buf, s_buf, c_buf, o_buf, sems):
    odd = lax.axis_index("strip") % 2
    rows = pl.ds(pl.multiple_of(24 * odd, 8), 40)
    bufs = (d_buf, s_buf, c_buf, o_buf)
    copies = [
        pltpu.make_async_copy(source.at[rows, :], buf, sems.at[i])
        for i, (source, buf) in enumerate(zip((density, speed, codes, obstacle), bufs))
    ]
    for item in copies:
        item.start()
    for item in copies:
        item.wait()
    for block in range(4):
        fields = products(*bufs, pl.ds(pl.multiple_of(8 * (block + odd), 8), 8))
        for field, tiles in enumerate(fields):
            for t, value in enumerate(tiles):
                sent[t, pl.ds(HALO * field + 8 * block, 8), :] = value
    rate, code, _ = products(*bufs, pl.ds(pl.multiple_of(32 * (1 - odd), 8), 8))
    for t in range(TILES):
        sent[t, pl.ds(3 * HALO, 8), :] = edge_tile(rate[t], code[t], odd == 1)


def own_kernel(density, speed, codes, obstacle, own, sent):
    even = lax.axis_index("strip") % 2 == 0
    for block in range(HEIGHT // 8):
        fields = products(density, speed, codes, obstacle, pl.ds(8 * block, 8))
        for field, tiles in enumerate(fields):
            for t, value in enumerate(interleave(tiles)):
                own[t, pl.ds(HEIGHT * field + 8 * block, 8), :] = value
    for t in range(TILES):
        for field in range(3):
            for block in range(4):
                first, second = (own[t, pl.ds(HEIGHT * field + 8 * b, 8), :] for b in (block, block + 4))
                sent[t, pl.ds(HALO * field + 8 * block, 8), :] = jnp.where(even, second, first)
        rate, code = (
            jnp.where(even, own[t, pl.ds(HEIGHT * field + 24, 8), :], own[t, pl.ds(HEIGHT * field + 32, 8), :])
            for field in range(2)
        )
        sent[t, pl.ds(3 * HALO, 8), :] = edge_tile(rate, code, even)


def from_left(tile):
    return pltpu.roll(tile, 1, 1)


def from_right(tile):
    return pltpu.roll(tile, LANES - 1, 1)


def from_above(tile):
    return jnp.where(sublane_ids() == 0, 0.0, pltpu.roll(tile, 1, 0))


def from_below(tile):
    return jnp.where(sublane_ids() == 7, 0.0, pltpu.roll(tile, 7, 0))


def sweep(rows, tiles, amounts_at, emit):
    sums = {}

    def add(r, t, value):
        sums[r, t] = sums[r, t] + value if (r, t) in sums else value

    def finish(r):
        add(r, 0, from_left(sums.pop((r, tiles))))
        add(r, tiles - 1, from_right(sums.pop((r, -1))))
        for t in range(tiles):
            emit(r, t, sums.pop((r, t)))

    for r in range(rows):
        for t in (*range(1, tiles - 1), 0, tiles - 1):
            kept, flows = amounts_at(r, t)
            if kept is not None:
                add(r, t, kept)
            for flow, (dr, dc) in zip(flows, OFFSETS):
                add(r + dr, t + dc, flow)
        if r == rows - 1:
            for t in range(-1, tiles + 1):
                add(0, t, from_above(sums.pop((rows, t))))
        if r == 0:
            for t in range(-1, tiles + 1):
                add(rows - 1, t, from_below(sums.pop((-1, t))))
        if r >= 2:
            finish(r - 1)
    finish(rows - 1)
    finish(0)


def picked(bits, values):
    for bit in bits:
        values = [jnp.where(bit, odd, even) for even, odd in zip(values[0::2], values[1::2])]
    return values[0]


SIDES = [[d for d, (_, dc) in enumerate(OFFSETS) if dc == step] for step in (1, -1)]


class Level:
    def __init__(self, first, rows, tiles, rate, parts, bits, weight, sides=None):
        self.first, self.rows, self.tiles, self.sides = first, rows, tiles, sides
        self.rate, self.parts, self.bits, self.weight = rate, parts, bits, weight

    def at(self, r, t):
        return r * self.tiles + t

    def cells(self):
        return [(r, t) for r in range(self.rows) for t in range(self.tiles)]

    def line(self, r):
        return pl.ds(self.first + r, 8, stride=self.rows)

    def get(self, ref, r, t):
        return ref[t, self.line(r), :]

    def put(self, ref, r, t, value):
        ref[t, self.line(r), :] = value

    def fill(self, rate_at, code_at, opening_at):
        opening = {}

        def amounts_at(r, t):
            rate, code = rate_at(r, t), code_at(r, t)
            opening[r, t] = opening_at(r, t)
            for side, column_step, lane in ((0, -1, 0), (self.tiles - 1, 1, LANES - 1)):
                if t == side:
                    for d, (_, dc) in enumerate(OFFSETS):
                        if dc == column_step:
                            code = jnp.where(code == jnp.where(lane_ids() == lane, float(d), -1.0), 8.0, code)
                    rate = jnp.where(code == 8.0, 0.0, rate)
            masks = [code == float(d) for d in range(8)]
            self.put(self.rate, r, t, rate)
            for d, mask in enumerate(masks):
                part = jnp.where(mask, rate, 0.0)
                self.put(self.parts.at[d], r, t, part)
                if self.sides is None:
                    continue
                if t == self.tiles - 1 and d in SIDES[0]:
                    self.sides[SIDES[0].index(d), self.line(r), :] = from_left(part)
                if t == 0 and d in SIDES[1]:
                    self.sides[3 + SIDES[1].index(d), self.line(r), :] = from_right(part)
            number = code.astype(jnp.int32)
            for n in range(3):
                self.put(self.bits.at[n], r, t, number & (1 << n))
            return None, [jnp.where(mask, opening[r, t], 0.0) for mask in masks]

        def emit(r, t, count):
            self.put(self.weight, r, t, opening[r, t] / jnp.maximum(count, 1.0))

        sweep(self.rows, self.tiles, amounts_at, emit)

    def advance(self, rho, base=0):
        (self.advance_rolling_sums if self.sides is None else self.advance_entering)(rho, base)

    def advance_rolling_sums(self, rho, base):
        rows, tiles = self.rows, self.tiles
        field, room = {}, {}

        def load(r):
            for t in range(tiles):
                field[r, t] = rho[base + self.at(r, t)]
                room[r, t] = (1.0 - field[r, t]) * self.get(self.weight, r, t)
            room[r, -1] = from_left(room[r, tiles - 1])
            room[r, tiles] = from_right(room[r, 0])

        def amounts_at(r, t):
            needed = [row for row in (r - 1, r, r + 1) if 0 <= row < rows] + [rows - 1] * (r == 0)
            for row in needed:
                if (row, 0) not in room:
                    load(row)
            if r == 0 and (-1, 0) not in room:
                for tt in range(-1, tiles + 1):
                    room[-1, tt] = from_above(room[rows - 1, tt])
            if r == rows - 1 and (rows, 0) not in room:
                for tt in range(-1, tiles + 1):
                    room[rows, tt] = from_below(room[0, tt])
            bits = [self.get(self.bits.at[n], r, t) != 0 for n in range(3)]
            leaving = picked(bits, [room[r + dr, t + dc] for dr, dc in OFFSETS])
            share = field[r, t] * leaving
            flows = [self.get(self.parts.at[d], r, t) * share for d in range(8)]
            return field[r, t] - self.get(self.rate, r, t) * share, flows

        def emit(r, t, value):
            rho[base + self.at(r, t)] = value

        sweep(rows, tiles, amounts_at, emit)

    def advance_entering(self, rho, base):
        rows, tiles = self.rows, self.tiles
        field, room, sums, entering = {}, {}, {}, {}

        def load(r):
            for t in range(tiles):
                field[r, t] = rho[base + self.at(r, t)]
                room[r, t] = (1.0 - field[r, t]) * self.get(self.weight, r, t)
            field[r, -1] = from_left(field[r, tiles - 1])
            field[r, tiles] = from_right(field[r, 0])
            room[r, -1] = from_left(room[r, tiles - 1])
            room[r, tiles] = from_right(room[r, 0])

        def add(target, key, value):
            target[key] = target[key] + value if key in target else value

        def finish(r):
            add(sums, (r, 0), room[r, 0] * entering.pop((r, 0)))
            add(sums, (r, tiles - 1), room[r, tiles - 1] * entering.pop((r, 1)))
            for t in range(tiles):
                rho[base + self.at(r, t)] = sums.pop((r, t))

        for r in range(rows):
            needed = [row for row in (r - 1, r, r + 1) if 0 <= row < rows] + [rows - 1] * (r == 0)
            for row in needed:
                if (row, 0) not in room:
                    load(row)
            if r == 0:
                for t in range(-1, tiles + 1):
                    room[-1, t] = from_above(room[rows - 1, t])
            if r == rows - 1:
                for t in range(-1, tiles + 1):
                    room[rows, t] = from_below(room[0, t])
            for t in (*range(1, tiles - 1), 0, tiles - 1):
                bits = [self.get(self.bits.at[n], r, t) != 0 for n in range(3)]
                leaving = picked(bits, [room[r + dr, t + dc] for dr, dc in OFFSETS])
                share = field[r, t] * leaving
                add(sums, (r, t), field[r, t] - self.get(self.rate, r, t) * share)
                for d, (dr, dc) in enumerate(OFFSETS):
                    if 0 <= t + dc < tiles:
                        add(sums, (r + dr, t + dc), self.get(self.parts.at[d], r, t) * share)
            for side, directions in enumerate(SIDES):
                for i, d in enumerate(directions):
                    pushed = self.sides[3 * side + i, self.line(r), :] * field[r, (-1, tiles)[side]]
                    add(entering, (r + OFFSETS[d][0], side), pushed)
            for row, target, moved in ((rows - 1, 0, from_above), (0, rows - 1, from_below)):
                if r == row:
                    beyond = rows if row else -1
                    for t in range(tiles):
                        add(sums, (target, t), moved(sums.pop((beyond, t))))
                    for side in range(2):
                        add(entering, (target, side), moved(entering.pop((beyond, side))))
            if r >= 2:
                finish(r - 1)
        finish(rows - 1)
        finish(0)


def halved(coarse, lines, change=lambda tile: tile):
    def at(r, t):
        upper, lower = (pl.ds(2 * (coarse.first + r) + i, 8, stride=2 * coarse.rows) for i in range(2))
        a, b, c, d = (
            change(lines[2 * t + j, rows, :]) for j, rows in ((0, upper), (0, lower), (1, upper), (1, lower))
        )
        return 0.25 * (((a + b) + c) + d)

    return {(r, t): at(r, t) for r, t in coarse.cells()}


def is_open(value):
    return jnp.where(value > 0.0, 1.0, 0.0)


def main_kernel(
    own, crossed, paired, out, rate, code, start, sending, parts, bits, weight, rho,
    crate, cparts, cbits, cweight, csides, pair, last_guess, result, sems,
):
    even = lax.axis_index("strip") % 2 == 0
    fields = (rate, code, start)
    for i, field in enumerate(fields):
        for t in range(TILES):
            for block in range(HEIGHT // 8):
                field[t, pl.ds(MARGIN + 8 * block, 8), :] = own[t, pl.ds(HEIGHT * i + 8 * block, 8), :]

    zeros = jnp.zeros((8, LANES), jnp.float32)

    def place_halo(tiles_at, high):
        place = pl.multiple_of(jnp.where(high, MARGIN + HEIGHT, MARGIN - HALO), 8)
        beyond = pl.ds(pl.multiple_of(jnp.where(high, SPAN - 8, 0), 8), 8)
        for i, field in enumerate(fields):
            for block in range(HALO // 8):
                for t, tile in enumerate(tiles_at(HALO * i + 8 * block)):
                    field[t, pl.ds(place + 8 * block, 8), :] = tile
        s = sublane_ids()
        for t, tile in enumerate(tiles_at(3 * HALO)):
            there = jnp.where(high, s, 7 - s) < 2
            turned = jnp.where(high, pltpu.roll(tile, 6, 0), pltpu.roll(tile, 2, 0))
            rate[t, beyond, :] = jnp.where(there, tile, 0.0)
            code[t, beyond, :] = jnp.where(there, turned, 0.0)
            start[t, beyond, :] = zeros

    place_halo(lambda row: [paired[t, pl.ds(row, 8), :] for t in range(TILES)], even)
    place_halo(
        lambda row: interleave([crossed[t, pl.ds(row, 8), :] for t in range(TILES)]), jnp.logical_not(even)
    )
    for field in fields:
        for t in range(TILES):
            field[t, pl.ds(SPAN, 8), :] = zeros

    stages = [
        (
            Level(*window, TILES, sending, parts, bits, weight),
            Level(*window_c, TILES_C, crate, cparts, cbits, cweight, csides),
        )
        for window, window_c in zip(STAGES, STAGES_C)
    ]
    fine, coarse = stages[0]
    openings = {}

    def rate_at(r, t):
        value = fine.get(rate, r, t)
        openings[r, t] = is_open(value)
        return value

    fine.fill(rate_at, lambda r, t: fine.get(code, r, t), lambda r, t: openings[r, t])
    mean_rate = halved(coarse, rate)
    mean_open = halved(coarse, rate, is_open)
    def coarse_code_at(r, t):
        return code[2 * t, pl.ds(2 * (coarse.first + r), 8, stride=2 * coarse.rows), :]

    coarse.fill(lambda r, t: mean_rate[r, t], coarse_code_at, lambda r, t: mean_open[r, t])

    n = lax.axis_index("tm")

    half = STAGES_C[0][1] * TILES_C

    for (r, t), value in halved(coarse, start).items():
        pair[coarse.at(r, t)] = value
    for r, t in fine.cells():
        rho[fine.at(r, t)] = fine.get(start, r, t)

    @pl.loop(0, CSTEPS)
    def _(step):
        fine.advance(rho)
        coarse.advance(pair)

    @pl.loop(CSTEPS, FINE)
    def _(step):
        fine.advance(rho)

    for r, t in coarse.cells():
        coarse.put(last_guess, r, t, pair[coarse.at(r, t)])
    for r, t in fine.cells():
        fine.put(start, r, t, rho[fine.at(r, t)])

    def stage(m):
        fine, coarse = stages[m]

        @pl.when(n >= m)
        def _():
            for (r, t), value in halved(coarse, start).items():
                pair[half + coarse.at(r, t)] = value
            for r, t in coarse.cells():
                value = coarse.get(last_guess, r, t)
                pair[coarse.at(r, t)] = value
                for i in range(4):
                    rho[fine.at(2 * r + i // 2, 2 * t + i % 2)] = value

            @pl.loop(0, FINE)
            def _(step):
                fine.advance(rho)
                coarse.advance(pair, half * (step // CSTEPS))

            for r, t in coarse.cells():
                value = pair[coarse.at(r, t)]
                change = pair[half + coarse.at(r, t)] - value
                coarse.put(last_guess, r, t, value)
                for i in range(4):
                    rr, tt = 2 * r + i // 2, 2 * t + i % 2
                    fine.put(start, rr, tt, rho[fine.at(rr, tt)] + change)

    for m in range(1, len(STAGES)):
        stage(m)

    copies = []
    for block in range(HEIGHT // 8):
        rows = pl.ds(MARGIN + 8 * block, 8)
        for j, value in enumerate(deinterleave([start[t, rows, :] for t in range(TILES)])):
            result[pl.ds(8 * block, 8), pl.ds(LANES * j, LANES)] = value
        if block % 2:
            rows = pl.ds(8 * (block - 1), 16)
            copies.append(pltpu.make_async_copy(result.at[rows, :], out.at[rows, :], sems.at[block // 2]))
            copies[-1].start()
    for item in copies:
        item.wait()


def per_device(density, speed, codes, obstacle):
    f32, i32 = jnp.float32, jnp.int32
    args = (density, speed, codes, obstacle)
    sent_shape = pltpu.VMEM((TILES, SENT, LANES), f32)
    to_cross = pl.pallas_call(
        cross_kernel,
        out_shape=sent_shape,
        in_specs=[pl.BlockSpec(memory_space=pl.ANY)] * 4,
        scratch_shapes=[pltpu.VMEM((40, TILES * LANES), x.dtype) for x in args] + [pltpu.SemaphoreType.DMA((4,))],
        name="cross",
    )(*args)
    count = lax.axis_size("strip")
    across = [(i, i + 1) for i in range(1, count - 1, 2)]
    within = [(i, i + 1) for i in range(0, count, 2)]
    crossed = lax.ppermute(to_cross, "strip", across + [(j, i) for i, j in across])
    own, to_pair = pl.pallas_call(
        own_kernel,
        out_shape=(pltpu.VMEM((TILES, 3 * HEIGHT, LANES), f32), sent_shape),
        cost_estimate=pl.CostEstimate(flops=10_000_000, bytes_accessed=2_000_000, transcendentals=0),
        name="own",
    )(*args)
    paired = lax.ppermute(to_pair, "strip", within + [(j, i) for i, j in within])

    fine_lines = (TILES, LINES, LANES)
    coarse_lines = (TILES_C, LINES_C, LANES)
    result = pl.pallas_call(
        main_kernel,
        out_shape=jax.ShapeDtypeStruct((HEIGHT, TILES * LANES), f32),
        in_specs=[pl.BlockSpec(memory_space=pltpu.VMEM)] * 3,
        scratch_shapes=[
            pltpu.VMEM(fine_lines, f32),
            pltpu.VMEM(fine_lines, f32),
            pltpu.VMEM(fine_lines, f32),
            pltpu.VMEM(fine_lines, f32),
            pltpu.VMEM((8, *fine_lines), f32),
            pltpu.VMEM((3, *fine_lines), i32),
            pltpu.VMEM(fine_lines, f32),
            pltpu.VMEM((STAGES[0][1] * TILES, 8, LANES), f32),
            pltpu.VMEM(coarse_lines, f32),
            pltpu.VMEM((8, *coarse_lines), f32),
            pltpu.VMEM((3, *coarse_lines), i32),
            pltpu.VMEM(coarse_lines, f32),
            pltpu.VMEM((6, *coarse_lines[1:]), f32),
            pltpu.VMEM((2 * STAGES_C[0][1] * TILES_C, 8, LANES), f32),
            pltpu.VMEM(coarse_lines, f32),
            pltpu.VMEM((HEIGHT, TILES * LANES), f32),
            pltpu.SemaphoreType.DMA((4,)),
        ],
        out_specs=pl.BlockSpec(memory_space=pl.ANY),
        compiler_params=pltpu.CompilerParams(vmem_limit_bytes=32 * 1024 * 1024),
        name="parareal",
    )(own, crossed, paired)
    return result[None]


def solution(mesh):
    in_specs = (P("strip", None), P("strip", None), P("strip", None), P("strip", None))
    out_specs = P("tm", "strip", None)
    return jax.shard_map(
        per_device, mesh=mesh, in_specs=in_specs, out_specs=out_specs, check_vma=False
    )
```

```python
import jax
import jax.numpy as jnp
from jax import lax
from jax.experimental import pallas as pl
from jax.experimental.pallas import tpu as pltpu
from jax.sharding import PartitionSpec as P

FINE = 8
CSTEPS = 4
LAMBDA = 0.9
OFFSETS = ((0, 1), (-1, 1), (-1, 0), (-1, -1), (0, -1), (1, -1), (1, 0), (1, 1))

LANES = 128
TILES = 4
TILES_C = TILES // 2
HEIGHT = 64
HALO = 32
MARGIN = 40
SPAN = HEIGHT + 2 * MARGIN
SENT = 3 * HALO + 8
STAGES = ((7, 17), (16, 14), (24, 12), (32, 10))
STAGES_C = ((3, 9), (8, 7), (12, 6), (16, 5))
LINES, LINES_C = 168, 88


def lane_ids():
    return lax.broadcasted_iota(jnp.int32, (8, LANES), 1)


def sublane_ids():
    return lax.broadcasted_iota(jnp.int32, (8, LANES), 0)


def exchange_blocks(tiles):
    lane = lane_ids()

    def swap(first, second, width):
        low = lane % (2 * width) < width
        return (
            jnp.where(low, first, pltpu.roll(second, width, 1)),
            jnp.where(low, pltpu.roll(first, LANES - width, 1), second),
        )

    a, b, c, d = tiles
    (a, c), (b, d) = swap(a, c, 64), swap(b, d, 64)
    return [*swap(a, b, 32), *swap(c, d, 32)]


def interleave(tiles):
    lane = lane_ids()
    index = TILES * (lane % 32) + lane // 32
    return exchange_blocks([jnp.take_along_axis(tile, index, axis=1) for tile in tiles])


def interleave_by_gathers(tiles):
    lane = lane_ids()
    result = []
    for t in range(TILES):
        index = (lane * TILES + t) % LANES
        picked = [jnp.take_along_axis(tile, index, axis=1) for tile in tiles]
        merged = picked[3]
        for j in (2, 1, 0):
            merged = jnp.where(lane < 32 * (j + 1), picked[j], merged)
        result.append(merged)
    return result


def deinterleave(tiles):
    lane = lane_ids()
    index = 32 * (lane % TILES) + lane // TILES
    return [jnp.take_along_axis(tile, index, axis=1) for tile in exchange_blocks(tiles)]


def products(density, speed, codes, obstacle, rows):
    cols = [pl.ds(LANES * j, LANES) for j in range(TILES)]
    opening = [1.0 - obstacle[rows, c].astype(jnp.float32) for c in cols]
    rate = [LAMBDA * speed[rows, c] * o for c, o in zip(cols, opening)]
    start = [density[rows, c] * o for c, o in zip(cols, opening)]
    code = [codes[rows, c].astype(jnp.float32) for c in cols]
    return rate, code, start


def edge_tile(rate, code, to_next):
    s = sublane_ids()
    below = jnp.where(s >= 6, rate, pltpu.roll(code, 6, 0))
    above = jnp.where(s < 2, rate, pltpu.roll(code, 2, 0))
    return jnp.where(to_next, below, above)


def cross_kernel(density, speed, codes, obstacle, sent, d_buf, s_buf, c_buf, o_buf, sems):
    odd = lax.axis_index("strip") % 2
    rows = pl.ds(pl.multiple_of(24 * odd, 8), 40)
    bufs = (d_buf, s_buf, c_buf, o_buf)
    copies = [
        pltpu.make_async_copy(source.at[rows, :], buf, sems.at[i])
        for i, (source, buf) in enumerate(zip((density, speed, codes, obstacle), bufs))
    ]
    for item in copies:
        item.start()
    for item in copies:
        item.wait()
    for block in range(4):
        fields = products(*bufs, pl.ds(pl.multiple_of(8 * (block + odd), 8), 8))
        for field, tiles in enumerate(fields):
            for t, value in enumerate(tiles):
                sent[t, pl.ds(HALO * field + 8 * block, 8), :] = value
    rate, code, _ = products(*bufs, pl.ds(pl.multiple_of(32 * (1 - odd), 8), 8))
    for t in range(TILES):
        sent[t, pl.ds(3 * HALO, 8), :] = edge_tile(rate[t], code[t], odd == 1)


def own_kernel(density, speed, codes, obstacle, own, sent):
    even = lax.axis_index("strip") % 2 == 0
    for block in range(HEIGHT // 8):
        fields = products(density, speed, codes, obstacle, pl.ds(8 * block, 8))
        for field, tiles in enumerate(fields):
            for t, value in enumerate(interleave_by_gathers(tiles)):
                own[t, pl.ds(HEIGHT * field + 8 * block, 8), :] = value
    for t in range(TILES):
        for field in range(3):
            for block in range(4):
                first, second = (own[t, pl.ds(HEIGHT * field + 8 * b, 8), :] for b in (block, block + 4))
                sent[t, pl.ds(HALO * field + 8 * block, 8), :] = jnp.where(even, second, first)
        rate, code = (
            jnp.where(even, own[t, pl.ds(HEIGHT * field + 24, 8), :], own[t, pl.ds(HEIGHT * field + 32, 8), :])
            for field in range(2)
        )
        sent[t, pl.ds(3 * HALO, 8), :] = edge_tile(rate, code, even)


def from_left(tile):
    return pltpu.roll(tile, 1, 1)


def from_right(tile):
    return pltpu.roll(tile, LANES - 1, 1)


def from_above(tile):
    return jnp.where(sublane_ids() == 0, 0.0, pltpu.roll(tile, 1, 0))


def from_below(tile):
    return jnp.where(sublane_ids() == 7, 0.0, pltpu.roll(tile, 7, 0))


def sweep(rows, tiles, amounts_at, emit):
    sums = {}

    def add(r, t, value):
        sums[r, t] = sums[r, t] + value if (r, t) in sums else value

    def finish(r):
        add(r, 0, from_left(sums.pop((r, tiles))))
        add(r, tiles - 1, from_right(sums.pop((r, -1))))
        for t in range(tiles):
            emit(r, t, sums.pop((r, t)))

    for r in range(rows):
        for t in (*range(1, tiles - 1), 0, tiles - 1):
            kept, flows = amounts_at(r, t)
            if kept is not None:
                add(r, t, kept)
            for flow, (dr, dc) in zip(flows, OFFSETS):
                add(r + dr, t + dc, flow)
        if r == rows - 1:
            for t in range(-1, tiles + 1):
                add(0, t, from_above(sums.pop((rows, t))))
        if r == 0:
            for t in range(-1, tiles + 1):
                add(rows - 1, t, from_below(sums.pop((-1, t))))
        if r >= 2:
            finish(r - 1)
    finish(rows - 1)
    finish(0)


def picked(bits, values):
    for bit in bits:
        values = [jnp.where(bit, odd, even) for even, odd in zip(values[0::2], values[1::2])]
    return values[0]


SIDES = [[d for d, (_, dc) in enumerate(OFFSETS) if dc == step] for step in (1, -1)]


class Level:
    def __init__(self, first, rows, tiles, rate, parts, bits, weight, sides=None):
        self.first, self.rows, self.tiles, self.sides = first, rows, tiles, sides
        self.rate, self.parts, self.bits, self.weight = rate, parts, bits, weight

    def at(self, r, t):
        return r * self.tiles + t

    def cells(self):
        return [(r, t) for r in range(self.rows) for t in range(self.tiles)]

    def line(self, r):
        return pl.ds(self.first + r, 8, stride=self.rows)

    def get(self, ref, r, t):
        return ref[t, self.line(r), :]

    def put(self, ref, r, t, value):
        ref[t, self.line(r), :] = value

    def fill(self, rate_at, code_at, opening_at):
        opening = {}

        def amounts_at(r, t):
            rate, code = rate_at(r, t), code_at(r, t)
            opening[r, t] = opening_at(r, t)
            for side, column_step, lane in ((0, -1, 0), (self.tiles - 1, 1, LANES - 1)):
                if t == side:
                    for d, (_, dc) in enumerate(OFFSETS):
                        if dc == column_step:
                            code = jnp.where(code == jnp.where(lane_ids() == lane, float(d), -1.0), 8.0, code)
                    rate = jnp.where(code == 8.0, 0.0, rate)
            masks = [code == float(d) for d in range(8)]
            self.put(self.rate, r, t, rate)
            for d, mask in enumerate(masks):
                part = jnp.where(mask, rate, 0.0)
                self.put(self.parts.at[d], r, t, part)
                if self.sides is None:
                    continue
                if t == self.tiles - 1 and d in SIDES[0]:
                    self.sides[SIDES[0].index(d), self.line(r), :] = from_left(part)
                if t == 0 and d in SIDES[1]:
                    self.sides[3 + SIDES[1].index(d), self.line(r), :] = from_right(part)
            number = code.astype(jnp.int32)
            for n in range(3):
                self.put(self.bits.at[n], r, t, number & (1 << n))
            return None, [jnp.where(mask, opening[r, t], 0.0) for mask in masks]

        def emit(r, t, count):
            self.put(self.weight, r, t, opening[r, t] / jnp.maximum(count, 1.0))

        sweep(self.rows, self.tiles, amounts_at, emit)

    def advance(self, rho, base=0):
        (self.advance_rolling_sums if self.sides is None else self.advance_entering)(rho, base)

    def advance_rolling_sums(self, rho, base):
        rows, tiles = self.rows, self.tiles
        field, room = {}, {}

        def load(r):
            for t in range(tiles):
                field[r, t] = rho[base + self.at(r, t)]
                room[r, t] = (1.0 - field[r, t]) * self.get(self.weight, r, t)
            room[r, -1] = from_left(room[r, tiles - 1])
            room[r, tiles] = from_right(room[r, 0])

        def amounts_at(r, t):
            needed = [row for row in (r - 1, r, r + 1) if 0 <= row < rows] + [rows - 1] * (r == 0)
            for row in needed:
                if (row, 0) not in room:
                    load(row)
            if r == 0 and (-1, 0) not in room:
                for tt in range(-1, tiles + 1):
                    room[-1, tt] = from_above(room[rows - 1, tt])
            if r == rows - 1 and (rows, 0) not in room:
                for tt in range(-1, tiles + 1):
                    room[rows, tt] = from_below(room[0, tt])
            bits = [self.get(self.bits.at[n], r, t) != 0 for n in range(3)]
            leaving = picked(bits, [room[r + dr, t + dc] for dr, dc in OFFSETS])
            share = field[r, t] * leaving
            flows = [self.get(self.parts.at[d], r, t) * share for d in range(8)]
            return field[r, t] - self.get(self.rate, r, t) * share, flows

        def emit(r, t, value):
            rho[base + self.at(r, t)] = value

        sweep(rows, tiles, amounts_at, emit)

    def advance_entering(self, rho, base):
        rows, tiles = self.rows, self.tiles
        field, room, sums, entering = {}, {}, {}, {}

        def load(r):
            for t in range(tiles):
                field[r, t] = rho[base + self.at(r, t)]
                room[r, t] = (1.0 - field[r, t]) * self.get(self.weight, r, t)
            field[r, -1] = from_left(field[r, tiles - 1])
            field[r, tiles] = from_right(field[r, 0])
            room[r, -1] = from_left(room[r, tiles - 1])
            room[r, tiles] = from_right(room[r, 0])

        def add(target, key, value):
            target[key] = target[key] + value if key in target else value

        def finish(r):
            add(sums, (r, 0), room[r, 0] * entering.pop((r, 0)))
            add(sums, (r, tiles - 1), room[r, tiles - 1] * entering.pop((r, 1)))
            for t in range(tiles):
                rho[base + self.at(r, t)] = sums.pop((r, t))

        for r in range(rows):
            needed = [row for row in (r - 1, r, r + 1) if 0 <= row < rows] + [rows - 1] * (r == 0)
            for row in needed:
                if (row, 0) not in room:
                    load(row)
            if r == 0:
                for t in range(-1, tiles + 1):
                    room[-1, t] = from_above(room[rows - 1, t])
            if r == rows - 1:
                for t in range(-1, tiles + 1):
                    room[rows, t] = from_below(room[0, t])
            for t in (*range(1, tiles - 1), 0, tiles - 1):
                bits = [self.get(self.bits.at[n], r, t) != 0 for n in range(3)]
                leaving = picked(bits, [room[r + dr, t + dc] for dr, dc in OFFSETS])
                share = field[r, t] * leaving
                add(sums, (r, t), field[r, t] - self.get(self.rate, r, t) * share)
                for d, (dr, dc) in enumerate(OFFSETS):
                    if 0 <= t + dc < tiles:
                        add(sums, (r + dr, t + dc), self.get(self.parts.at[d], r, t) * share)
            for side, directions in enumerate(SIDES):
                for i, d in enumerate(directions):
                    pushed = self.sides[3 * side + i, self.line(r), :] * field[r, (-1, tiles)[side]]
                    add(entering, (r + OFFSETS[d][0], side), pushed)
            for row, target, moved in ((rows - 1, 0, from_above), (0, rows - 1, from_below)):
                if r == row:
                    beyond = rows if row else -1
                    for t in range(tiles):
                        add(sums, (target, t), moved(sums.pop((beyond, t))))
                    for side in range(2):
                        add(entering, (target, side), moved(entering.pop((beyond, side))))
            if r >= 2:
                finish(r - 1)
        finish(rows - 1)
        finish(0)


def halved(coarse, lines, change=lambda tile: tile):
    def at(r, t):
        upper, lower = (pl.ds(2 * (coarse.first + r) + i, 8, stride=2 * coarse.rows) for i in range(2))
        a, b, c, d = (
            change(lines[2 * t + j, rows, :]) for j, rows in ((0, upper), (0, lower), (1, upper), (1, lower))
        )
        return 0.25 * (((a + b) + c) + d)

    return {(r, t): at(r, t) for r, t in coarse.cells()}


def is_open(value):
    return jnp.where(value > 0.0, 1.0, 0.0)


def main_kernel(
    own, crossed, paired, out, rate, code, start, sending, parts, bits, weight, rho,
    crate, cparts, cbits, cweight, csides, pair, last_guess, result, sems,
):
    even = lax.axis_index("strip") % 2 == 0
    fields = (rate, code, start)
    for i, field in enumerate(fields):
        for t in range(TILES):
            for block in range(HEIGHT // 8):
                field[t, pl.ds(MARGIN + 8 * block, 8), :] = own[t, pl.ds(HEIGHT * i + 8 * block, 8), :]

    zeros = jnp.zeros((8, LANES), jnp.float32)

    def place_halo(tiles_at, high):
        place = pl.multiple_of(jnp.where(high, MARGIN + HEIGHT, MARGIN - HALO), 8)
        beyond = pl.ds(pl.multiple_of(jnp.where(high, SPAN - 8, 0), 8), 8)
        for i, field in enumerate(fields):
            for block in range(HALO // 8):
                for t, tile in enumerate(tiles_at(HALO * i + 8 * block)):
                    field[t, pl.ds(place + 8 * block, 8), :] = tile
        s = sublane_ids()
        for t, tile in enumerate(tiles_at(3 * HALO)):
            there = jnp.where(high, s, 7 - s) < 2
            turned = jnp.where(high, pltpu.roll(tile, 6, 0), pltpu.roll(tile, 2, 0))
            rate[t, beyond, :] = jnp.where(there, tile, 0.0)
            code[t, beyond, :] = jnp.where(there, turned, 0.0)
            start[t, beyond, :] = zeros

    place_halo(lambda row: [paired[t, pl.ds(row, 8), :] for t in range(TILES)], even)
    place_halo(
        lambda row: interleave([crossed[t, pl.ds(row, 8), :] for t in range(TILES)]), jnp.logical_not(even)
    )
    for field in fields:
        for t in range(TILES):
            field[t, pl.ds(SPAN, 8), :] = zeros

    stages = [
        (
            Level(*window, TILES, sending, parts, bits, weight),
            Level(*window_c, TILES_C, crate, cparts, cbits, cweight, csides),
        )
        for window, window_c in zip(STAGES, STAGES_C)
    ]
    fine, coarse = stages[0]
    openings = {}

    def rate_at(r, t):
        value = fine.get(rate, r, t)
        openings[r, t] = is_open(value)
        return value

    fine.fill(rate_at, lambda r, t: fine.get(code, r, t), lambda r, t: openings[r, t])
    mean_rate = halved(coarse, rate)
    mean_open = halved(coarse, rate, is_open)
    def coarse_code_at(r, t):
        return code[2 * t, pl.ds(2 * (coarse.first + r), 8, stride=2 * coarse.rows), :]

    coarse.fill(lambda r, t: mean_rate[r, t], coarse_code_at, lambda r, t: mean_open[r, t])

    n = lax.axis_index("tm")

    half = STAGES_C[0][1] * TILES_C

    for (r, t), value in halved(coarse, start).items():
        pair[coarse.at(r, t)] = value
    for r, t in fine.cells():
        rho[fine.at(r, t)] = fine.get(start, r, t)

    @pl.loop(0, CSTEPS)
    def _(step):
        fine.advance(rho)
        coarse.advance(pair)

    @pl.loop(CSTEPS, FINE)
    def _(step):
        fine.advance(rho)

    for r, t in coarse.cells():
        coarse.put(last_guess, r, t, pair[coarse.at(r, t)])
    for r, t in fine.cells():
        fine.put(start, r, t, rho[fine.at(r, t)])

    def stage(m):
        fine, coarse = stages[m]

        @pl.when(n >= m)
        def _():
            for (r, t), value in halved(coarse, start).items():
                pair[half + coarse.at(r, t)] = value
            for r, t in coarse.cells():
                value = coarse.get(last_guess, r, t)
                pair[coarse.at(r, t)] = value
                for i in range(4):
                    rho[fine.at(2 * r + i // 2, 2 * t + i % 2)] = value

            @pl.loop(0, FINE)
            def _(step):
                fine.advance(rho)
                coarse.advance(pair, half * (step // CSTEPS))

            for r, t in coarse.cells():
                value = pair[coarse.at(r, t)]
                change = pair[half + coarse.at(r, t)] - value
                coarse.put(last_guess, r, t, value)
                for i in range(4):
                    rr, tt = 2 * r + i // 2, 2 * t + i % 2
                    fine.put(start, rr, tt, rho[fine.at(rr, tt)] + change)

    for m in range(1, len(STAGES)):
        stage(m)

    copies = []
    for block in range(HEIGHT // 8):
        rows = pl.ds(MARGIN + 8 * block, 8)
        for j, value in enumerate(deinterleave([start[t, rows, :] for t in range(TILES)])):
            result[pl.ds(8 * block, 8), pl.ds(LANES * j, LANES)] = value
        if block % 2:
            rows = pl.ds(8 * (block - 1), 16)
            copies.append(pltpu.make_async_copy(result.at[rows, :], out.at[rows, :], sems.at[block // 2]))
            copies[-1].start()
    for item in copies:
        item.wait()


def per_device(density, speed, codes, obstacle):
    f32, i32 = jnp.float32, jnp.int32
    args = (density, speed, codes, obstacle)
    sent_shape = pltpu.VMEM((TILES, SENT, LANES), f32)
    to_cross = pl.pallas_call(
        cross_kernel,
        out_shape=sent_shape,
        in_specs=[pl.BlockSpec(memory_space=pl.ANY)] * 4,
        scratch_shapes=[pltpu.VMEM((40, TILES * LANES), x.dtype) for x in args] + [pltpu.SemaphoreType.DMA((4,))],
        name="cross",
    )(*args)
    count = lax.axis_size("strip")
    across = [(i, i + 1) for i in range(1, count - 1, 2)]
    within = [(i, i + 1) for i in range(0, count, 2)]
    crossed = lax.ppermute(to_cross, "strip", across + [(j, i) for i, j in across])
    own, to_pair = pl.pallas_call(
        own_kernel,
        out_shape=(pltpu.VMEM((TILES, 3 * HEIGHT, LANES), f32), sent_shape),
        cost_estimate=pl.CostEstimate(flops=10_000_000, bytes_accessed=2_000_000, transcendentals=0),
        name="own",
    )(*args)
    paired = lax.ppermute(to_pair, "strip", within + [(j, i) for i, j in within])

    fine_lines = (TILES, LINES, LANES)
    coarse_lines = (TILES_C, LINES_C, LANES)
    result = pl.pallas_call(
        main_kernel,
        out_shape=jax.ShapeDtypeStruct((HEIGHT, TILES * LANES), f32),
        in_specs=[pl.BlockSpec(memory_space=pltpu.VMEM)] * 3,
        scratch_shapes=[
            pltpu.VMEM(fine_lines, f32),
            pltpu.VMEM(fine_lines, f32),
            pltpu.VMEM(fine_lines, f32),
            pltpu.VMEM(fine_lines, f32),
            pltpu.VMEM((8, *fine_lines), f32),
            pltpu.VMEM((3, *fine_lines), i32),
            pltpu.VMEM(fine_lines, f32),
            pltpu.VMEM((STAGES[0][1] * TILES, 8, LANES), f32),
            pltpu.VMEM(coarse_lines, f32),
            pltpu.VMEM((8, *coarse_lines), f32),
            pltpu.VMEM((3, *coarse_lines), i32),
            pltpu.VMEM(coarse_lines, f32),
            pltpu.VMEM((6, *coarse_lines[1:]), f32),
            pltpu.VMEM((2 * STAGES_C[0][1] * TILES_C, 8, LANES), f32),
            pltpu.VMEM(coarse_lines, f32),
            pltpu.VMEM((HEIGHT, TILES * LANES), f32),
            pltpu.SemaphoreType.DMA((4,)),
        ],
        out_specs=pl.BlockSpec(memory_space=pl.ANY),
        compiler_params=pltpu.CompilerParams(vmem_limit_bytes=32 * 1024 * 1024),
        name="parareal",
    )(own, crossed, paired)
    return result[None]


def solution(mesh):
    in_specs = (P("strip", None), P("strip", None), P("strip", None), P("strip", None))
    out_specs = P("tm", "strip", None)
    return jax.shard_map(
        per_device, mesh=mesh, in_specs=in_specs, out_specs=out_specs, check_vma=False
    )
```
